128 devices in a mesh: dom: 16 (over y_hi, x, core), rep: 8 (over z, y_lo).
Axes of the slice: x: 4, y: 4 (y_hi: 2, y_lo: 2; y = y_hi * 2 + y_lo), z: 4, core: 2. Of those that a mesh axis runs over, the one named last changes fastest.
Arguments:
- features: bfloat16 [24576, 256], P(('dom', 'rep')), may hold values from -6 to 6
- weight: bfloat16 [256, 256], replicated, may hold values from -0.375 to 0.375
- bias: float32 [256], replicated, may hold values from -3 to 3
- adj_tiles: bfloat16 [192, 16, 8, 128, 128], P('dom', None, 'rep'), may hold values from -0.078125 to 0.078125
- adj_cols: int32 [192, 16, 8], P('dom', None, 'rep'), may hold values from 0 to 11, as said below
- degree: int32 [192, 16], P('dom'), may hold values from 1 to 8, as said below
- grad_out: bfloat16 [24576, 256], P(('dom', 'rep')), may hold values from -6 to 6
Outputs:
- activated: bfloat16 [24576, 256], P(('dom', 'rep'))
- feature_grad: bfloat16 [24576, 256], P(('dom', 'rep'))
- weight_grad: float32 [256, 256], replicated
- bias_grad: float32 [256], replicated
The draws below stay inside these ranges and needn't reach their ends.
Inputs may be any that keep to these rules, and one draw needn't show every extreme that they name: `degree`: in every source shard column some block row uses all 8 slots; most block rows use fewer, and low slots are used more often than high ones. `adj_cols`: within one block row and one source shard the 8 entries are distinct.
All inputs are finite; a program needn't handle non-finite values.
Results may differ from the reference program's by a relative error of at most 0.018.
Values may be sent and summed in bfloat16 or wider, within the bound.
A program may use at most 128 MiB of HBM per device.

```python
import math
import jax
import jax.numpy as jnp
from jax import lax

BLK = 128
F = 256
BD = 12
SLOTS = 8
NB = 192
ROWS = 24576
N_DOM = 16


def draw_degree(key, part):
    key = jax.random.fold_in(key, 7)
    first_key, second_key, third_key = jax.random.split(key, 3)
    first_draw = jax.random.randint(first_key, (NB, N_DOM), 1, SLOTS + 1)
    second_draw = jax.random.randint(second_key, (NB, N_DOM), 1, SLOTS + 1)
    lowest = jnp.minimum(first_draw, second_draw)
    hub_rows = jax.random.randint(third_key, (N_DOM,), 0, NB)
    row_ids = jnp.arange(NB, dtype=jnp.int32)[:, None]
    return jnp.where(row_ids == hub_rows[None, :], SLOTS, lowest).astype(jnp.int32)


def draw_adj_cols(key, part):
    key = jax.random.fold_in(key, 11)
    scores = jax.random.randint(key, (NB, N_DOM, BD), 0, 1048576)
    distinct = scores * BD + jnp.arange(BD, dtype=jnp.int32)[None, None, :]
    order = jnp.argsort(distinct, axis=-1, stable=True)
    return order[:, :, :SLOTS].astype(jnp.int32)


def block_scale(stream_key, extent, shards, low, largest):
    factor_of = 1.0
    for axis_at, parts in shards:
        steps = jax.random.uniform(jax.random.fold_in(jax.random.fold_in(stream_key, 6), axis_at), (parts,), jnp.float32, low / len(shards), largest / len(shards))
        factor_of = factor_of * jnp.repeat(jnp.exp(steps), extent[axis_at] // parts).reshape((-1,) + (1,) * (len(extent) - 1 - axis_at))
    return factor_of


def scatter_about(stream_key, shape, scale, bound, shards=(), kind=jnp.bfloat16):
    values = scale * jax.random.normal(stream_key, shape, jnp.float32)
    if shards:
        values = values * block_scale(stream_key, shape, shards, -0.22, 0.18)
    return jnp.clip(values, -bound, bound).astype(kind)


def setup_inputs(seed: int = 0) -> dict:
    splits = jax.random.split(jax.random.key(seed), 8)
    return {
        "features": scatter_about(splits[0], (ROWS, F), 1.0, 6.0, ((0, 128),)),
        "weight": scatter_about(splits[1], (F, F), F ** -0.5, 0.375),
        "bias": scatter_about(splits[2], (F,), 0.5, 3.0, (), jnp.float32),
        "adj_tiles": scatter_about(splits[3], (NB, N_DOM, SLOTS, BLK, BLK), (BLK * N_DOM * SLOTS // 3) ** -0.5, 0.078125, ((0, 16), (2, 8))),
        "adj_cols": draw_adj_cols(jax.random.fold_in(splits[7], 71), 0),
        "degree": draw_degree(jax.random.fold_in(splits[7], 71), 0),
        "grad_out": scatter_about(splits[6], (ROWS, F), 1.0, 6.0, ((0, 128),)),
    }


def masked(adj_tiles, degree):
    slot_ids = jnp.arange(SLOTS, dtype=jnp.int32)
    used_mask = (slot_ids[None, None, :] < degree[:, :, None]).astype(adj_tiles.dtype)
    return adj_tiles * used_mask[:, :, :, None, None]

def smooth_gate(inputs):
    return jax.nn.gelu(inputs, approximate=True)

def reference(features, weight, bias, adj_tiles, adj_cols, degree, grad_out):
    tile_vals = masked(adj_tiles, degree)
    feature_blocks = features.reshape(NB, BLK, F)
    shard_base = (jnp.arange(N_DOM, dtype=jnp.int32) * BD)[:, None]

    def row_block(pair):
        block_tiles, block_cols = pair
        selected = feature_blocks[shard_base + block_cols.astype(jnp.int32)]
        return jnp.einsum('jkxy,jkyf->xf', block_tiles.astype(jnp.float32), selected.astype(jnp.float32))
    aggregated = lax.map(row_block, (tile_vals, adj_cols)).reshape(ROWS, F).astype(jnp.bfloat16)
    preact = jnp.dot(aggregated, weight, preferred_element_type=jnp.float32) + bias
    activated, pullback = jax.vjp(smooth_gate, preact)
    delta = pullback(grad_out.astype(jnp.float32))[0].astype(jnp.bfloat16)
    grad_scale = 1.0 / math.sqrt(ROWS)
    weight_grad = jnp.dot(aggregated.T, delta, preferred_element_type=jnp.float32) * grad_scale
    bias_grad = lax.optimization_barrier(jnp.sum(delta.astype(jnp.float32), axis=0)) * grad_scale
    spread = jnp.dot(delta, weight.T, preferred_element_type=jnp.float32).astype(jnp.bfloat16)
    spread_blocks = spread.reshape(NB, BLK, F)

    def back_block(running, triple):
        block_tiles, block_cols, source = triple
        product = jnp.einsum('jkxy,xf->jkyf', block_tiles.astype(jnp.float32), source.astype(jnp.float32))
        return (running.at[shard_base + block_cols.astype(jnp.int32)].add(product), None)
    running, unused = lax.scan(back_block, jnp.zeros((NB, BLK, F), jnp.float32), (tile_vals, adj_cols, spread_blocks))
    feature_grad = running.reshape(ROWS, F).astype(jnp.bfloat16)
    return (activated.astype(jnp.bfloat16), feature_grad, weight_grad, bias_grad)
```

```python
import math

import jax
import jax.numpy as jnp
from jax import lax
from jax.experimental import pallas as pl
from jax.experimental.pallas import tpu as pltpu
from jax.sharding import PartitionSpec as P

MESH = pl.DeviceIdType.MESH
BF16, F32, I32 = jnp.bfloat16, jnp.float32, jnp.int32
RING, SIDE = 4, 64
BLOCKS, SHARDS, EDGE, HID = 12, 8, 128, 256
CHUNK = 192
REPS, DOMS = 8, 16
NONE = BLOCKS
ROOT = math.sqrt(2.0 / math.pi)
CUBIC = 0.044715


def wrap(value, size):
    return lax.rem(value, size)


def place(part, x, y, z):
    at = (x, y, z)
    return part * 64 + at[(part + 2) % 3] * 16 + at[(part + 1) % 3] * 4 + at[part]


def kernel(scale, feat, weight, bias, tiles, meta, grad_out,
           act_out, fgrad_out, wgrad_out, bgrad_out,
           own, swapped, flipped, table_in, table, gathered,
           theirs, arrived, mine, shares, landed, spread,
           chain, grads, lands_c, lands_b, lands_a,
           wterm, wland, wdom, wall,
           ag_send, ag_recv, rs_send, rs_recv, core_send, core_recv, local_sem,
           rep_send, rep_recv, spr_send, spr_recv, fwd_send, fwd_recv,
           w1_send, w1_recv, w2_send, w2_recv, w3_send, w3_recv):
    dom, rep = lax.axis_index("dom"), lax.axis_index("rep")
    core = wrap(dom, 2)
    x = wrap(lax.div(dom, 2), 4)
    y_hi = lax.div(dom, 8)
    z, y_lo = lax.div(rep, 2), wrap(rep, 2)
    y = y_hi * 2 + y_lo
    at = (x, y, z)

    def device(px, py, pz, pc):
        return ((lax.div(py, 2) * 4 + px) * 2 + pc, pz * 2 + wrap(py, 2))

    def near(axis, step):
        to = list(at)
        to[axis] = wrap(at[axis] + step, RING)
        return device(*to, core)

    partner = (dom + 1 - 2 * core, rep)

    barrier = pltpu.get_barrier_semaphore()
    for k in range(1, REPS):
        pl.semaphore_signal(barrier, inc=1, device_id=(dom, wrap(rep + k, REPS)), device_id_type=MESH)
    for k in range(1, DOMS):
        pl.semaphore_signal(barrier, inc=1, device_id=(wrap(dom + k, DOMS), rep), device_id_type=MESH)
    for step in (1, 3):
        pl.semaphore_signal(barrier, inc=1, device_id=near(1, step), device_id_type=MESH)
    pl.semaphore_wait(barrier, REPS - 1 + DOMS - 1 + 2)

    started = []

    def send(src, dst, send_sem, recv_sem, target):
        copy = pltpu.make_async_remote_copy(
            src_ref=src, dst_ref=dst, send_sem=send_sem, recv_sem=recv_sem, device_id=target, device_id_type=MESH)
        copy.start()
        started.append(copy)
        return copy

    def half(ref, phase, part, e, h):
        axis = (at[part], at[(part + 1) % 3], at[(part + 2) % 3])
        if phase == 0:
            return ref.at[part * 64 + axis[2] * 16 + axis[1] * 4 + e, pl.ds(32 * h, 32)]
        if phase == 1:
            return ref.at[pl.ds(part * 64 + axis[2] * 16 + e * 4 + 2 * h, 2)]
        return ref.at[pl.ds(part * 64 + e * 16 + 8 * h, 8)]

    def ag_sem(phase, part, way, k):
        return ((phase * 3 + part) * 2 + way) * 3 + k

    def ag_copy(phase, part, way, k, go):
        axis = (part + phase) % 3
        m = at[axis]
        target = near(axis, 1 if way == 0 else 3)
        sem = ag_sem(phase, part, way, k)
        if go:
            e = m if k < 2 else wrap(m + (3 if way == 0 else 1), RING)
        else:
            back = (3 if way == 0 else 1) * (1 if k < 2 else 2)
            e = wrap(m + back, RING)
        h = way if k in (0, 2) else 1 - way
        ref = half(gathered, phase, part, e, h)
        if go:
            send(ref, ref, ag_send.at[sem], ag_recv.at[sem], target)
        else:
            pltpu.make_async_remote_copy(
                src_ref=ref, dst_ref=ref, send_sem=ag_send.at[sem], recv_sem=ag_recv.at[sem],
                device_id=target, device_id_type=MESH).wait_recv()

    def ag_each(phase, k, go):
        for part in range(3):
            for way in range(2):
                ag_copy(phase, part, way, k, go)

    def flip(which, first, count):
        def body(b, carry):
            for s in range(SHARDS):
                flipped[which, b, pl.ds(s * EDGE, EDGE), :] = jnp.transpose(swapped[which, b * SHARDS + s])
            return carry
        lax.fori_loop(first, first + count, body, 0)

    for part in range(3):
        gathered[place(part, x, y, z)] = feat[pl.ds(part * SIDE, SIDE), :]
    gathered[192] = jnp.zeros((SIDE, HID), BF16)
    ag_each(0, 0, True)
    ag_each(0, 1, True)
    table_copy = send(meta.at[1 - core], table_in, core_send.at[0], core_recv.at[0], partner)
    tile_copy = send(tiles.at[:, 1 - core], swapped.at[1], core_send.at[1], core_recv.at[1], partner)
    own_table = pltpu.make_async_copy(meta.at[core], table.at[0], local_sem.at[0])
    own_table.start()
    own_tiles = pltpu.make_async_copy(tiles.at[:, core], swapped.at[0], local_sem.at[1])
    own_tiles.start()
    ag_each(0, 0, False)
    ag_each(0, 2, True)
    own_tiles.wait()
    flip(0, 0, 1)
    ag_each(0, 1, False)
    ag_each(0, 2, False)
    ag_each(1, 0, True)
    ag_each(1, 1, True)
    flip(0, 1, 2)
    ag_each(1, 0, False)
    ag_each(1, 2, True)
    flip(0, 3, 2)
    ag_each(1, 1, False)
    ag_each(1, 2, False)
    ag_each(2, 0, True)
    ag_each(2, 1, True)
    flip(0, 5, 6)
    ag_each(2, 0, False)
    ag_each(2, 2, True)
    own_table.wait()
    table_copy.wait_recv()
    their_table = pltpu.make_async_copy(table_in, table.at[1], local_sem.at[2])
    their_table.start()
    flip(0, 11, 1)
    tile_copy.wait_recv()
    flip(1, 0, 12)
    their_table.wait()
    ag_each(2, 1, False)
    ag_each(2, 2, False)

    def row_block(which, b):
        lhs = jnp.concatenate([swapped[which, b * SHARDS + s] for s in range(SHARDS)], axis=1)
        rhs = jnp.concatenate([gathered[table[which, b, k]] for k in range(2 * SHARDS)], axis=0)
        return jnp.dot(lhs, rhs, preferred_element_type=F32)

    def their_block(b, carry):
        theirs[pl.ds(pl.multiple_of(b * EDGE, EDGE), EDGE), :] = row_block(1, b).astype(BF16)
        return carry

    def my_block(b, carry):
        mine[pl.ds(pl.multiple_of(b * EDGE, EDGE), EDGE), :] = row_block(0, b)
        return carry

    swap = []
    for part in range(4):
        lax.fori_loop(part * 3, part * 3 + 3, their_block, 0)
        rows = pl.ds(part * 384, 384)
        swap.append(send(theirs.at[rows], arrived.at[rows], core_send.at[2 + part], core_recv.at[2 + part], partner))
    lax.fori_loop(0, BLOCKS, my_block, 0)
    for copy in swap:
        copy.wait_recv()

    def rows_of(peer):
        return pl.ds(pl.multiple_of(peer * CHUNK, CHUNK), CHUNK)

    slots = []
    for k in range(1, REPS):
        to = wrap(rep + k, REPS)
        rows = rows_of(to)
        shares[to] = (mine[rows, :] + arrived[rows, :].astype(F32)).astype(BF16)
        slots.append(send(shares.at[to], landed.at[rep], rep_send.at[k], rep_recv.at[k], (dom, to)))
    total = mine[rows_of(rep), :] + arrived[rows_of(rep), :].astype(F32)
    for k in range(1, REPS):
        slots[k - 1].wait_recv()
        total = total + landed[wrap(rep + REPS - k, REPS)].astype(F32)

    aggregated = total.astype(BF16)
    v = jnp.dot(aggregated, weight[...], preferred_element_type=F32) + bias[...]
    t = jnp.tanh(ROOT * (v + CUBIC * (v * v * v)))
    act_out[...] = (0.5 * v * (1.0 + t)).astype(BF16)
    slope = 0.5 * (1.0 + t) + 0.5 * v * ((1.0 - t) * (1.0 + t)) * (ROOT * (1.0 + 3.0 * CUBIC * (v * v)))
    delta = (grad_out[...].astype(F32) * slope).astype(BF16)
    spread[0, rows_of(rep), :] = lax.dot_general(
        delta, weight[...], (((1,), (1,)), ((), ())), preferred_element_type=F32).astype(BF16)
    here = spread.at[0, rows_of(rep)]
    spread_in = []
    for k in range(1, REPS):
        spread_in.append(send(here, here, spr_send.at[k], spr_recv.at[k], (dom, wrap(rep + k, REPS))))
    forward_in = [send(here, spread.at[1, rows_of(rep)], fwd_send.at[0], fwd_recv.at[0], partner)]

    wsum = lax.dot_general(aggregated, delta, (((0,), (0,)), ((), ())), preferred_element_type=F32)
    bsum = jnp.sum(delta.astype(F32).reshape(CHUNK // 8, 8, HID), axis=0)
    for r in range(REPS):
        wterm[r, 0:32, :] = wsum[r * 32:(r + 1) * 32, :]
        wterm[r, 32:40, :] = bsum
    wland[rep] = wterm[rep]

    for k in range(1, REPS):
        spread_in[k - 1].wait_recv()
        rows = rows_of(wrap(rep + REPS - k, REPS))
        forward_in.append(send(spread.at[0, rows], spread.at[1, rows], fwd_send.at[k], fwd_recv.at[k], partner))
    w1 = []
    for k in range(1, REPS):
        to = wrap(rep + k, REPS)
        w1.append(send(wterm.at[to], wland.at[rep], w1_send.at[k], w1_recv.at[k], (dom, to)))

    for s in range(2):
        for which in range(2):
            chain[s, which * 13 + NONE] = jnp.zeros((EDGE, HID), F32)

    def link(g, which):
        def body(b, carry):
            rows = pl.ds(pl.multiple_of(g * 2 * EDGE, 2 * EDGE), 2 * EDGE)
            product = jnp.dot(
                flipped[which, b, rows, :], spread[which, pl.ds(pl.multiple_of(b * EDGE, EDGE), EDGE), :],
                preferred_element_type=F32)
            for s in range(2):
                before = table[which, b, 2 * SHARDS + g * 2 + s]
                chain[s, which * 13 + b] = product[s * EDGE:(s + 1) * EDGE] + chain[s, which * 13 + before]
            return carry
        lax.fori_loop(0, BLOCKS, body, 0)

    def close(g):
        for s in range(2):
            shard = g * 2 + s
            sy, sx = lax.div(shard, 4), wrap(shard, 4)
            for c in range(BLOCKS):
                both = (chain[s, table[0, c, 3 * SHARDS + shard]]
                        + chain[s, 13 + table[1, c, 3 * SHARDS + shard]]).astype(BF16)
                for h in range(2):
                    q = 2 * c + h
                    r = q // 3
                    grads[place(q % 3, sx, sy * 2 + r % 2, r // 2)] = both[h * SIDE:(h + 1) * SIDE]

    link(0, 0)
    for copy in forward_in:
        copy.wait_recv()
    link(0, 1)
    close(0)

    def shard_pair(g, carry):
        link(g, 0)
        link(g, 1)
        close(g)
        return carry

    lax.fori_loop(1, 4, shard_pair, 0)

    for copy in w1:
        copy.wait_recv()
    wdom[dom] = sum(wland[r] for r in range(REPS))
    w2 = []
    for k in range(1, DOMS):
        w2.append(send(wdom.at[dom], wdom.at[dom], w2_send.at[k], w2_recv.at[k], (wrap(dom + k, DOMS), rep)))

    lands = (lands_a, lands_b, lands_c)

    def rs_copy(phase, part, way, k, go):
        axis = (part + phase) % 3
        m = at[axis]
        sem = ag_sem(phase, part, way, k)
        e = wrap(m + (2 if k == 0 else (1 if way == 0 else 3)), RING)
        h = way if k in (0, 2) else 1 - way
        land = lands[phase].at[(part * 2 + way) * 3 + k]
        target = near(axis, 1 if way == 0 else 3)
        if go:
            send(half(grads, phase, part, e, h), land, rs_send.at[sem], rs_recv.at[sem], target)
        else:
            pltpu.make_async_remote_copy(
                src_ref=land, dst_ref=land, send_sem=rs_send.at[sem], recv_sem=rs_recv.at[sem],
                device_id=target, device_id_type=MESH).wait_recv()

    def rs_each(phase, k, go):
        for part in range(3):
            for way in range(2):
                rs_copy(phase, part, way, k, go)

    def reduce(phase):
        rs_each(phase, 0, True)
        rs_each(phase, 1, True)
        for part in range(3):
            for way in range(2):
                axis = (part + phase) % 3
                rs_copy(phase, part, way, 0, False)
                to = half(grads, phase, part, wrap(at[axis] + (1 if way == 0 else 3), RING), way)
                to[...] = (to[...].astype(F32)
                           + lands[phase][(part * 2 + way) * 3].astype(F32)).astype(BF16)
                rs_copy(phase, part, way, 2, True)

    def settle(phase):
        for part in range(3):
            axis = (part + phase) % 3
            for way in range(2):
                rs_copy(phase, part, way, 1, False)
            for way in range(2):
                rs_copy(phase, part, way, 2, False)
            for h in range(2):
                ref = half(grads, phase, part, at[axis], h)
                full = (ref[...].astype(F32) + lands[phase][(part * 2 + h) * 3 + 2].astype(F32)
                        + lands[phase][(part * 2 + 1 - h) * 3 + 1].astype(F32)).astype(BF16)
                if phase == 0:
                    fgrad_out[pl.ds(part * SIDE + 32 * h, 32), :] = full
                else:
                    ref[...] = full

    reduce(2)
    settle(2)

    for copy in w2:
        copy.wait_recv()
    wfull = sum(wdom[d] for d in range(DOMS)) * scale
    wall[rep] = wfull[0:32]
    bgrad_out[...] = jnp.sum(wfull[32:40], axis=0, keepdims=True)
    w3 = []
    for k in range(1, REPS):
        w3.append(send(wall.at[rep], wall.at[rep], w3_send.at[k], w3_recv.at[k], (dom, wrap(rep + k, REPS))))

    reduce(1)
    settle(1)
    reduce(0)
    settle(0)
    for copy in w3:
        copy.wait_recv()
    for r in range(REPS):
        wgrad_out[pl.ds(r * 32, 32), :] = wall[r]
    for copy in started:
        copy.wait_send()


def tables(adj_cols, degree):
    rep = lax.axis_index("rep")
    cols = adj_cols[:, :, 0]
    used = rep < degree
    shard = jnp.arange(SHARDS, dtype=I32)[None, :, None, None]
    half = jnp.arange(2, dtype=I32)[None, None, None, :]
    q = 2 * cols.reshape(BLOCKS, SHARDS, 2, 1) + half
    part, r = q % 3, q // 3
    x, y, z = shard % 4 + 0 * r, (shard // 4) * 2 + r % 2, r // 2
    where = jnp.where(
        part == 0, place(0, x, y, z), jnp.where(part == 1, place(1, x, y, z), place(2, x, y, z)))
    where = jnp.where(used.reshape(BLOCKS, SHARDS, 2, 1), where, 192)
    where = where.transpose(2, 0, 1, 3).reshape(2, BLOCKS, 2 * SHARDS)
    blocks = jnp.arange(BLOCKS, dtype=I32)
    same = (cols[:, None, :] == cols[None, :, :]) & used[None, :, :] & (blocks[None, :, None] < blocks[:, None, None])
    before = jnp.max(jnp.where(same, blocks[None, :, None], -1), axis=1)
    hit = (cols[None, :, :] == blocks[:, None, None]) & used[None, :, :]
    last = jnp.max(jnp.where(hit, blocks[None, :, None], -1), axis=1)
    ends = [jnp.where(a < 0, NONE, a).reshape(BLOCKS, SHARDS, 2).transpose(2, 0, 1) for a in (before, last)]
    meta = jnp.concatenate([where] + ends, axis=2).astype(I32)
    return jnp.pad(meta, ((0, 0), (0, 4), (0, 96)))


def body(features, weight, bias, adj_tiles, adj_cols, degree, grad_out):
    vmem = pl.BlockSpec(memory_space=pltpu.VMEM)
    dma = pltpu.SemaphoreType.DMA
    rows = BLOCKS * EDGE
    scale = 1.0 / math.sqrt(CHUNK * REPS * DOMS)
    call = pl.pallas_call(
        lambda *refs: kernel(scale, *refs),
        out_shape=(
            jax.ShapeDtypeStruct((CHUNK, HID), BF16),
            jax.ShapeDtypeStruct((CHUNK, HID), BF16),
            jax.ShapeDtypeStruct((HID, HID), F32),
            jax.ShapeDtypeStruct((1, HID), F32),
        ),
        in_specs=[vmem, vmem, vmem, pl.BlockSpec(memory_space=pl.ANY), vmem, vmem],
        out_specs=(vmem, vmem, vmem, vmem),
        scratch_shapes=[
            pltpu.VMEM((8, 128), F32),
            pltpu.VMEM((2, BLOCKS * SHARDS, EDGE, EDGE), BF16),
            pltpu.VMEM((2, BLOCKS, SHARDS * EDGE, EDGE), BF16),
            pltpu.VMEM((16, 128), I32),
            pltpu.SMEM((2, 16, 128), I32),
            pltpu.VMEM((193, SIDE, HID), BF16),
            pltpu.VMEM((rows, HID), BF16),
            pltpu.VMEM((rows, HID), BF16),
            pltpu.VMEM((rows, HID), F32),
            pltpu.VMEM((REPS, CHUNK, HID), BF16),
            pltpu.VMEM((REPS, CHUNK, HID), BF16),
            pltpu.VMEM((2, rows, HID), BF16),
            pltpu.VMEM((2, 26, EDGE, HID), F32),
            pltpu.VMEM((192, SIDE, HID), BF16),
            pltpu.VMEM((18, 8, SIDE, HID), BF16),
            pltpu.VMEM((18, 2, SIDE, HID), BF16),
            pltpu.VMEM((18, 32, HID), BF16),
            pltpu.VMEM((REPS, 40, HID), F32),
            pltpu.VMEM((REPS, 40, HID), F32),
            pltpu.VMEM((DOMS, 40, HID), F32),
            pltpu.VMEM((REPS, 32, HID), F32),
            dma((54,)), dma((54,)), dma((54,)), dma((54,)), dma((6,)), dma((6,)), dma((3,)),
            dma((REPS,)), dma((REPS,)), dma((REPS,)), dma((REPS,)), dma((REPS,)), dma((REPS,)),
            dma((REPS,)), dma((REPS,)), dma((DOMS,)), dma((DOMS,)), dma((REPS,)), dma((REPS,)),
        ],
        compiler_params=pltpu.CompilerParams(
            collective_id=0, has_side_effects=True, vmem_limit_bytes=56 * 1024 * 1024),
    )
    act, fgrad, wgrad, bgrad = call(
        features, weight, bias.reshape(1, HID),
        adj_tiles.reshape(BLOCKS * SHARDS, 2, EDGE, EDGE), tables(adj_cols, degree), grad_out)
    return act, fgrad, wgrad, bgrad.reshape(HID)


def solution(mesh):
    return jax.shard_map(
        body,
        mesh=mesh,
        in_specs=(
            P(("dom", "rep"), None),
            P(),
            P(),
            P("dom", None, "rep", None, None),
            P("dom", None, "rep"),
            P("dom", None),
            P(("dom", "rep"), None),
        ),
        out_specs=(P(("dom", "rep"), None), P(("dom", "rep"), None), P(), P()),
        check_vma=False,
    )
```

```python
import math

import jax
import jax.numpy as jnp
from jax import lax
from jax.experimental import pallas as pl
from jax.experimental.pallas import tpu as pltpu
from jax.sharding import PartitionSpec as P

MESH = pl.DeviceIdType.MESH
BF16, F32, I32 = jnp.bfloat16, jnp.float32, jnp.int32
RING, SIDE = 4, 64
BLOCKS, SHARDS, EDGE, HID = 12, 8, 128, 256
CHUNK = 192
REPS = 8
NONE = BLOCKS
EMPTY = 192
ROOT = math.sqrt(2.0 / math.pi)
CUBIC = 0.044715


def wrap(value, size):
    return lax.rem(value, size)


def turned(part, x, y, z):
    at = (x, y, z)
    return at[(part + 2) % 3], at[(part + 1) % 3], at[part]


def place(part, x, y, z):
    c, b, a = turned(part, x, y, z)
    return part * 64 + c * 16 + b * 4 + a


def kernel(scale, feat, weight_in, bias_in, tiles, cols_in, degree_in, grad_in,
           act_out, fgrad_out, wgrad_out, bgrad_out,
           weight, bias, cols, degree, grad, act, fgrad,
           swapped, flipped, table_own, table_in, table, gathered,
           theirs, arrived, mine, shares, landed, spread,
           chain, grads, land_z, land_y, land_x, land_1, land_0,
           wterm, wx, wcore_out, wcore, whi_out, whi, wrep, wall, bsum_out,
           sems):
    dom, rep = lax.axis_index("dom"), lax.axis_index("rep")
    core = wrap(dom, 2)
    x = wrap(lax.div(dom, 2), 4)
    y_hi = lax.div(dom, 8)
    z, y_lo = lax.div(rep, 2), wrap(rep, 2)
    y = y_hi * 2 + y_lo
    at = (x, y, z)

    def near(axis, step):
        to = list(at)
        to[axis] = wrap(at[axis] + step, RING)
        return (lax.div(to[1], 2) * 4 + to[0]) * 2 + core, to[2] * 2 + wrap(to[1], 2)

    def peer(k):
        return dom, wrap(rep + k, REPS)

    partner = (dom + 1 - 2 * core, rep)
    across = (wrap(dom + 8, 16), rep)

    barrier = pltpu.get_barrier_semaphore()

    def greet(target):
        pl.semaphore_signal(barrier, inc=1, device_id=target, device_id_type=MESH)

    for axis in range(3):
        for step in (1, 3, 2):
            greet(near(axis, step))
    greet(partner)
    for k in range(1, REPS):
        greet(peer(k))

    used = [0]
    started = []

    def lane(count=1):
        used[0] += count
        return used[0] - count

    def local(src, dst):
        copy = pltpu.make_async_copy(src, dst, sems.at[lane()])
        copy.start()
        return copy

    def remote(src, dst, target, slot=None):
        slot = lane(2) if slot is None else slot
        return pltpu.make_async_remote_copy(
            src_ref=src, dst_ref=dst, send_sem=sems.at[slot], recv_sem=sems.at[slot + 1],
            device_id=target, device_id_type=MESH)

    def send(src, dst, target, slot=None):
        copy = remote(src, dst, target, slot)
        copy.start()
        started.append(copy)
        return copy

    small = [local(cols_in, cols), local(degree_in, degree)]
    pieces = [local(feat.at[pl.ds(part * SIDE, SIDE)], gathered.at[place(part, x, y, z)]) for part in range(3)]
    own_tiles = local(tiles.at[:, core], swapped.at[0])
    dense_in = [local(weight_in, weight), local(bias_in, bias), local(grad_in, grad)]
    gathered[EMPTY] = jnp.zeros((SIDE, HID), BF16)

    pl.semaphore_wait(barrier, 9 + 1 + REPS - 1)

    def row_of(part, c, b):
        return gathered.at[pl.ds(part * 64 + c * 16 + b * 4, 4)]

    def half_of(part, b, h):
        return gathered.at[pl.ds(part * 64 + at[(part + 2) % 3] * 16 + b * 4 + 2 * h, 2)]

    first = []
    for part in range(3):
        for step in (1, 3, 2):
            first.append(send(feat.at[pl.ds(part * SIDE, SIDE)], gathered.at[place(part, x, y, z)], near(part, step)))
    tile_copy = send(tiles.at[:, 1 - core], swapped.at[1], partner)

    for copy in small:
        copy.wait()
    col = cols[:, 0, :]
    live = rep < degree[...]
    shard = lax.div(lax.broadcasted_iota(I32, (BLOCKS, 16), 1), 2)
    shard_x, shard_y = wrap(shard, 4), lax.div(shard, 4) * 2
    block = lax.broadcasted_iota(I32, (BLOCKS, 16), 0)
    table_own[...] = jnp.zeros(table_own.shape, I32)
    for h in range(2):
        q = 2 * col + h
        r = (q * 11) >> 5
        part, to_z = q - 3 * r, r >> 1
        to_y = shard_y + (r - 2 * to_z)
        spot = jnp.where(part == 0, place(0, shard_x, to_y, to_z),
                         jnp.where(part == 1, place(1, shard_x, to_y, to_z), place(2, shard_x, to_y, to_z)))
        table_own[16 * h:16 * h + BLOCKS, 0:16] = jnp.where(live, spot, EMPTY)
    before = jnp.full((BLOCKS, 16), NONE, I32)
    last = jnp.full((BLOCKS, 16), NONE, I32)
    for b in range(BLOCKS):
        here = live[b:b + 1]
        before = jnp.where((col == col[b:b + 1]) & here & (block > b), b, before)
        last = jnp.where((block == col[b:b + 1]) & here, b, last)
    table_own[32:32 + BLOCKS, 0:16] = before
    table_own[48:48 + BLOCKS, 0:16] = last
    table_copy = send(table_own, table_in, partner)
    own_table = local(table_own, table.at[0])

    def flip(which, b0, count):
        def body(b, carry):
            for s in range(SHARDS):
                spot = (s % 4) * 2 + s // 4
                flipped[which, b, pl.ds(spot * EDGE, EDGE), :] = jnp.transpose(swapped[which, b * SHARDS + s])
            return carry
        lax.fori_loop(b0, b0 + count, body, 0)

    for copy in pieces:
        copy.wait()
    for copy in first:
        copy.wait_recv()

    slots_1 = [[[lane(2) for k in range(3)] for way in range(2)] for part in range(3)]
    slots_2 = [[[lane(2) for k in range(6)] for way in range(2)] for part in range(3)]
    FIRST, SECOND = (0, 1), (3, 2)

    def ways():
        for part in range(3):
            for way in range(2):
                yield part, way, (1 if way == 0 else 3)

    def round_1(part, way, step, k, go):
        m = at[(part + 1) % 3]
        h = way if k in (0, 2) else 1 - way
        if go:
            b = m if k < 2 else wrap(m + 4 - step, RING)
        else:
            b = wrap(m + (4 - step) * (1 if k < 2 else 2), RING)
        ref = half_of(part, b, h)
        target, slot = near((part + 1) % 3, step), slots_1[part][way][k]
        if go:
            send(ref, ref, target, slot)
        else:
            remote(ref, ref, target, slot).wait_recv()

    def round_2(part, way, step, k, go):
        m, b0 = at[(part + 2) % 3], at[(part + 1) % 3]
        offset = k if k < 4 else (FIRST if way == 0 else SECOND)[k - 4]
        if go:
            c = m if k < 4 else wrap(m + 4 - step, RING)
        else:
            c = wrap(m + (4 - step) * (1 if k < 4 else 2), RING)
        ref = row_of(part, c, wrap(b0 + offset, RING))
        target, slot = near((part + 2) % 3, step), slots_2[part][way][k]
        if go:
            send(ref, ref, target, slot)
        else:
            remote(ref, ref, target, slot).wait_recv()

    def each(action, k, go):
        for part, way, step in ways():
            action(part, way, step, k, go)

    each(round_1, 0, True)
    each(round_1, 1, True)
    each(round_2, 0, True)
    own_tiles.wait()
    flip(0, 0, 1)
    each(round_1, 0, False)
    each(round_1, 2, True)
    each(round_1, 1, False)
    each(round_2, 1, True)
    each(round_2, 3, True)
    flip(0, 1, 1)
    each(round_2, 0, False)
    for part, way, step in ways():
        if way == 0:
            round_2(part, way, step, 4, True)
    each(round_1, 2, False)
    each(round_2, 2, True)
    flip(0, 2, 4)
    each(round_2, 1, False)
    each(round_2, 3, False)
    for part, way, step in ways():
        if way == 0:
            round_2(part, way, step, 5, True)
        else:
            round_2(part, way, step, 4, True)
    flip(0, 6, 6)
    own_table.wait()
    table_copy.wait_recv()
    their_table = local(table_in, table.at[1])
    tile_copy.wait_recv()
    each(round_2, 2, False)
    for part, way, step in ways():
        if way == 1:
            round_2(part, way, step, 5, True)
    flip(1, 0, 12)
    their_table.wait()
    each(round_2, 4, False)
    each(round_2, 5, False)

    def entry(which, kind, b, s):
        return table[which, kind * 16 + b, 2 * s + core]

    def row_block(which, b):
        lhs = jnp.concatenate([swapped[which, b * SHARDS + s] for s in range(SHARDS)], axis=1)
        rhs = jnp.concatenate([gathered[entry(which, h, b, s)] for s in range(SHARDS) for h in range(2)], axis=0)
        return jnp.dot(lhs, rhs, preferred_element_type=F32)

    def their_block(b, carry):
        theirs[pl.ds(pl.multiple_of(b * EDGE, EDGE), EDGE), :] = row_block(1, b).astype(BF16)
        return carry

    def my_block(b, carry):
        mine[pl.ds(pl.multiple_of(b * EDGE, EDGE), EDGE), :] = row_block(0, b)
        return carry

    swap = []
    for part in range(4):
        lax.fori_loop(part * 3, part * 3 + 3, their_block, 0)
        rows = pl.ds(part * 384, 384)
        swap.append(send(theirs.at[rows], arrived.at[rows], partner))
    lax.fori_loop(0, BLOCKS, my_block, 0)
    for copy in swap:
        copy.wait_recv()

    def rows_of(r):
        return pl.ds(pl.multiple_of(r * CHUNK, CHUNK), CHUNK)

    slots = []
    for k in range(1, REPS):
        to = wrap(rep + k, REPS)
        rows = rows_of(to)
        shares[to] = (mine[rows, :] + arrived[rows, :].astype(F32)).astype(BF16)
        slots.append(send(shares.at[to], landed.at[rep], peer(k)))
    total = mine[rows_of(rep), :] + arrived[rows_of(rep), :].astype(F32)
    for copy in dense_in:
        copy.wait()
    for k in range(1, REPS):
        slots[k - 1].wait_recv()
        total = total + landed[wrap(rep + REPS - k, REPS)].astype(F32)

    aggregated = total.astype(BF16)
    v = jnp.dot(aggregated, weight[...], preferred_element_type=F32) + bias[...]
    t = jnp.tanh(ROOT * (v + CUBIC * (v * v * v)))
    slope = 0.5 * (1.0 + t) + 0.5 * v * ((1.0 - t) * (1.0 + t)) * (ROOT * (1.0 + 3.0 * CUBIC * (v * v)))
    delta = (grad[...].astype(F32) * slope).astype(BF16)
    spread[0, rows_of(rep), :] = lax.dot_general(
        delta, weight[...], (((1,), (1,)), ((), ())), preferred_element_type=F32).astype(BF16)
    here = spread.at[0, rows_of(rep)]
    spread_in = [send(here, here, peer(k)) for k in range(1, REPS)]
    forward_in = [send(here, spread.at[1, rows_of(rep)], partner)]
    act[...] = (0.5 * v * (1.0 + t)).astype(BF16)
    outgoing = [local(act, act_out)]

    wsum = lax.dot_general(aggregated, delta, (((0,), (0,)), ((), ())), preferred_element_type=F32)
    bsum = jnp.sum(delta.astype(F32).reshape(CHUNK // 8, 8, HID), axis=0)
    for k in range(RING):
        wterm[k, 0:64, :] = wsum[k * 64:(k + 1) * 64, :]
        wterm[k, 64:72, :] = bsum
    wx[x] = wterm[x]
    w_x = [send(wterm.at[wrap(x + k, RING)], wx.at[x], near(0, k)) for k in range(1, RING)]

    for k in range(1, REPS):
        spread_in[k - 1].wait_recv()
        rows = rows_of(wrap(rep + REPS - k, REPS))
        forward_in.append(send(spread.at[0, rows], spread.at[1, rows], partner))

    for s in range(2):
        for which in range(2):
            chain[s, which * 13 + NONE] = jnp.zeros((EDGE, HID), F32)

    def link(to_x, which):
        rows = pl.ds(pl.multiple_of(to_x * 2 * EDGE, 2 * EDGE), 2 * EDGE)

        def body(b, carry):
            product = jnp.dot(
                flipped[which, b, rows, :], spread[which, pl.ds(pl.multiple_of(b * EDGE, EDGE), EDGE), :],
                preferred_element_type=F32)
            for s in range(2):
                prior = chain[s, which * 13 + entry(which, 2, b, s * 4 + to_x)]
                chain[s, which * 13 + b] = product[s * EDGE:(s + 1) * EDGE] + prior
            return carry
        lax.fori_loop(0, BLOCKS, body, 0)

    def close(to_x):
        for s in range(2):
            for c in range(BLOCKS):
                both = (chain[s, entry(0, 3, c, s * 4 + to_x)]
                        + chain[s, 13 + entry(1, 3, c, s * 4 + to_x)]).astype(BF16)
                for h in range(2):
                    q = 2 * c + h
                    part, r = q % 3, q // 3
                    grads[(part,) + turned(part, to_x, s * 2 + r % 2, r // 2)] = both[h * SIDE:(h + 1) * SIDE]

    def add_to(ref, *others):
        full = ref[...].astype(F32)
        for other in others:
            full = full + other[...].astype(F32)
        ref[...] = full.astype(BF16)

    slots_q = [[[[lane(2) for k in range(3)] for way in range(2)] for g in range(4)] for part in (0, 2)]
    lands_q = {0: land_z, 2: land_y}

    def quarter(part, plane, to_x, h):
        if part == 0:
            return grads.at[0, plane, pl.ds(2 * h, 2), to_x]
        return grads.at[2, plane, to_x, pl.ds(2 * h, 2)]

    def quarter_copy(part, way, g, k, to_x):
        axis = 2 if part == 0 else 1
        step = 1 if way == 0 else 3
        plane = wrap(at[axis] + (2 if k == 0 else step), RING)
        h = way if k in (0, 2) else 1 - way
        return remote(quarter(part, plane, to_x, h), lands_q[part].at[(g * 2 + way) * 3 + k],
                      near(axis, step), slots_q[part // 2][g][way][k])

    def begin(copy):
        copy.start()
        started.append(copy)

    def quarter_send(g, to_x):
        for k in range(2):
            for part in (0, 2):
                for way in range(2):
                    begin(quarter_copy(part, way, g, k, to_x))

    def quarter_pass(g, to_x):
        for part in (0, 2):
            axis = 2 if part == 0 else 1
            for way in range(2):
                quarter_copy(part, way, g, 0, to_x).wait_recv()
                plane = wrap(at[axis] + (1 if way == 0 else 3), RING)
                add_to(quarter(part, plane, to_x, way), lands_q[part].at[(g * 2 + way) * 3])
                begin(quarter_copy(part, way, g, 2, to_x))

    def quarter_settle(g, to_x):
        for part in (0, 2):
            axis = 2 if part == 0 else 1
            for way in range(2):
                for k in (1, 2):
                    quarter_copy(part, way, g, k, to_x).wait_recv()
            for h in range(2):
                add_to(quarter(part, at[axis], to_x, h), lands_q[part].at[(g * 2 + h) * 3 + 2],
                       lands_q[part].at[(g * 2 + 1 - h) * 3 + 1])

    slots_x = [[lane(2) for k in range(3)] for way in range(2)]

    def plane_copy(way, k):
        step = 1 if way == 0 else 3
        h = way if k in (0, 2) else 1 - way
        return remote(grads.at[1, wrap(x + (2 if k == 0 else step), RING), pl.ds(2 * h, 2)], land_x.at[way * 3 + k],
                      near(0, step), slots_x[way][k])

    def plane_pass(way):
        begin(plane_copy(way, 1))
        plane_copy(way, 0).wait_recv()
        add_to(grads.at[1, wrap(x + (1 if way == 0 else 3), RING), pl.ds(2 * way, 2)], land_x.at[way * 3])
        begin(plane_copy(way, 2))

    def rows_out(part):
        axis = (part + 1) % 3
        out = []
        for k in range(1, RING):
            out.append(send(grads.at[part, at[(part + 2) % 3], wrap(at[axis] + k, RING)], land_1.at[part * 3 + k - 1],
                            near(axis, k)))
        return out

    def rows_in(part, copies):
        for copy in copies:
            copy.wait_recv()
        add_to(grads.at[part, at[(part + 2) % 3], at[(part + 1) % 3]], *[land_1.at[part * 3 + k] for k in range(3)])

    def piece_at(part, a):
        return grads.at[part, at[(part + 2) % 3], at[(part + 1) % 3], a]

    def pieces_out(part):
        return [send(piece_at(part, wrap(at[part] + k, RING)), land_0.at[part * 3 + k - 1], near(part, k))
                for k in range(1, RING)]

    def pieces_in(part, copies):
        for copy in copies:
            copy.wait_recv()
        full = piece_at(part, at[part])[...].astype(F32)
        for k in range(3):
            full = full + land_0[part * 3 + k].astype(F32)
        fgrad[pl.ds(part * SIDE, SIDE), :] = full.astype(BF16)

    turn = [wrap(x + 2, RING), wrap(x + 1, RING), wrap(x + 3, RING), x]

    link(turn[0], 0)
    for copy in forward_in:
        copy.wait_recv()
    link(turn[0], 1)
    close(turn[0])
    quarter_send(0, turn[0])
    begin(plane_copy(0, 0))
    begin(plane_copy(1, 0))
    for copy in w_x:
        copy.wait_recv()
    wsum = wx[0] + wx[1] + wx[2] + wx[3]
    wx[0] = wsum
    wcore_out[0:32, :] = wx[0, pl.ds(pl.multiple_of((1 - core) * 32, 32), 32), :]
    wcore_out[32:40, :] = wx[0, 64:72, :]
    w_core = send(wcore_out, wcore, partner)

    link(turn[1], 0)
    link(turn[1], 1)
    close(turn[1])
    quarter_pass(0, turn[0])
    quarter_send(1, turn[1])
    plane_pass(0)
    w_core.wait_recv()
    wcore[0:32, :] = wcore[0:32, :] + wx[0, pl.ds(pl.multiple_of(core * 32, 32), 32), :]
    wcore[32:40, :] = wcore[32:40, :] + wx[0, 64:72, :]
    whi_out[0:16, :] = wcore[pl.ds(pl.multiple_of((1 - y_hi) * 16, 16), 16), :]
    whi_out[16:24, :] = wcore[32:40, :]
    w_hi = send(whi_out, whi, across)

    link(turn[2], 0)
    link(turn[2], 1)
    close(turn[2])
    quarter_pass(1, turn[1])
    quarter_send(2, turn[2])
    plane_pass(1)
    quarter_settle(0, turn[0])
    w_hi.wait_recv()
    wrep[rep, 0:16, :] = whi[0:16, :] + wcore[pl.ds(pl.multiple_of(y_hi * 16, 16), 16), :]
    wrep[rep, 16:24, :] = whi[16:24, :] + wcore[32:40, :]
    w_rep = [send(wrep.at[rep], wrep.at[rep], peer(k)) for k in range(1, REPS)]

    link(turn[3], 0)
    link(turn[3], 1)
    close(turn[3])
    quarter_send(3, turn[3])
    quarter_pass(2, turn[2])
    quarter_settle(1, turn[1])
    for copy in w_rep:
        copy.wait_recv()
    wfull = wrep[0]
    for r in range(1, REPS):
        wfull = wfull + wrep[r]
    wfull = wfull * scale
    bsum_out[...] = jnp.sum(wfull[16:24], axis=0, keepdims=True)
    outgoing.append(local(bsum_out, bgrad_out))

    def wrows(start, count):
        return wall.at[pl.ds(pl.multiple_of(start, 16), count)]

    wall[pl.ds(pl.multiple_of(x * 64 + core * 32 + y_hi * 16, 16), 16), :] = wfull[0:16]
    ref = wrows(x * 64 + core * 32 + y_hi * 16, 16)
    w_hi = send(ref, ref, across)
    quarter_pass(3, turn[3])
    quarter_settle(2, turn[2])
    w_hi.wait_recv()
    ref = wrows(x * 64 + core * 32, 32)
    w_core = send(ref, ref, partner)

    for way in range(2):
        for k in (1, 2):
            plane_copy(way, k).wait_recv()
    for h in range(2):
        add_to(grads.at[1, x, pl.ds(2 * h, 2)], land_x.at[h * 3 + 2], land_x.at[(1 - h) * 3 + 1])
    rows = {1: rows_out(1)}
    quarter_settle(3, turn[3])
    for part in (0, 2):
        rows[part] = rows_out(part)
    w_core.wait_recv()
    ref = wrows(x * 64, 64)
    w_x = [send(ref, ref, near(0, k)) for k in range(1, RING)]
    last_out = {}
    for part in (1, 0, 2):
        rows_in(part, rows[part])
        last_out[part] = pieces_out(part)
    for copy in w_x:
        copy.wait_recv()
    outgoing.append(local(wall, wgrad_out))
    for part in (1, 0, 2):
        pieces_in(part, last_out[part])
    outgoing.append(local(fgrad, fgrad_out))
    for copy in started:
        copy.wait_send()
    for copy in outgoing:
        copy.wait()


def hand_over(*refs):
    ins, outs, held, sems = refs[:4], refs[4:8], refs[8:12], refs[12]
    copies = [pltpu.make_async_copy(ins[k], held[k], sems.at[k]) for k in range(4)]
    for copy in copies:
        copy.start()
    onward = []
    for k in range(4):
        copies[k].wait()
        onward.append(pltpu.make_async_copy(held[k], outs[k], sems.at[4 + k]))
        onward[k].start()
    for copy in onward:
        copy.wait()


def body(features, weight, bias, adj_tiles, adj_cols, degree, grad_out):
    anywhere = pl.BlockSpec(memory_space=pl.ANY)
    rows = BLOCKS * EDGE
    scale = 1.0 / math.sqrt(CHUNK * REPS * 16)
    outs = (
        jax.ShapeDtypeStruct((CHUNK, HID), BF16),
        jax.ShapeDtypeStruct((CHUNK, HID), BF16),
        jax.ShapeDtypeStruct((HID, HID), F32),
        jax.ShapeDtypeStruct((1, HID), F32),
    )
    call = pl.pallas_call(
        lambda *refs: kernel(scale, *refs),
        out_shape=outs,
        in_specs=[anywhere] * 7,
        out_specs=(anywhere,) * 4,
        scratch_shapes=[
            pltpu.VMEM((HID, HID), BF16),
            pltpu.VMEM((1, HID), F32),
            pltpu.VMEM((BLOCKS, 1, 16), I32),
            pltpu.VMEM((BLOCKS, 16), I32),
            pltpu.VMEM((CHUNK, HID), BF16),
            pltpu.VMEM((CHUNK, HID), BF16),
            pltpu.VMEM((CHUNK, HID), BF16),
            pltpu.VMEM((2, BLOCKS * SHARDS, EDGE, EDGE), BF16),
            pltpu.VMEM((2, BLOCKS, SHARDS * EDGE, EDGE), BF16),
            pltpu.VMEM((64, 128), I32),
            pltpu.VMEM((64, 128), I32),
            pltpu.SMEM((2, 64, 128), I32),
            pltpu.VMEM((193, SIDE, HID), BF16),
            pltpu.VMEM((rows, HID), BF16),
            pltpu.VMEM((rows, HID), BF16),
            pltpu.VMEM((rows, HID), F32),
            pltpu.VMEM((REPS, CHUNK, HID), BF16),
            pltpu.VMEM((REPS, CHUNK, HID), BF16),
            pltpu.VMEM((2, rows, HID), BF16),
            pltpu.VMEM((2, 26, EDGE, HID), F32),
            pltpu.VMEM((3, 4, 4, 4, SIDE, HID), BF16),
            pltpu.VMEM((24, 2, SIDE, HID), BF16),
            pltpu.VMEM((24, 2, SIDE, HID), BF16),
            pltpu.VMEM((6, 2, 4, SIDE, HID), BF16),
            pltpu.VMEM((9, 4, SIDE, HID), BF16),
            pltpu.VMEM((9, SIDE, HID), BF16),
            pltpu.VMEM((RING, 72, HID), F32),
            pltpu.VMEM((RING, 72, HID), F32),
            pltpu.VMEM((40, HID), F32),
            pltpu.VMEM((40, HID), F32),
            pltpu.VMEM((24, HID), F32),
            pltpu.VMEM((24, HID), F32),
            pltpu.VMEM((REPS, 24, HID), F32),
            pltpu.VMEM((HID, HID), F32),
            pltpu.VMEM((1, HID), F32),
            pltpu.SemaphoreType.DMA((512,)),
        ],
        compiler_params=pltpu.CompilerParams(
            collective_id=0, has_side_effects=True, vmem_limit_bytes=56 * 1024 * 1024),
    )
    results = call(
        features, weight, bias.reshape(1, HID),
        adj_tiles.reshape(BLOCKS * SHARDS, 2, EDGE, EDGE), adj_cols.transpose(0, 2, 1), degree, grad_out)
    act, fgrad, wgrad, bgrad = pl.pallas_call(
        hand_over,
        out_shape=outs,
        in_specs=[anywhere] * 4,
        out_specs=(anywhere,) * 4,
        scratch_shapes=[pltpu.VMEM(out.shape, out.dtype) for out in outs] + [pltpu.SemaphoreType.DMA((8,))],
    )(*results)
    return act, fgrad, wgrad, bgrad.reshape(HID)


def solution(mesh):
    return jax.shard_map(
        body,
        mesh=mesh,
        in_specs=(
            P(("dom", "rep"), None),
            P(),
            P(),
            P("dom", None, "rep", None, None),
            P("dom", None, "rep"),
            P("dom", None),
            P(("dom", "rep"), None),
        ),
        out_specs=(P(("dom", "rep"), None), P(("dom", "rep"), None), P(), P()),
        check_vma=False,
    )
```

```python
import math

import jax
import jax.numpy as jnp
from jax import lax
from jax.experimental import pallas as pl
from jax.experimental.pallas import tpu as pltpu
from jax.sharding import PartitionSpec as P

MESH = pl.DeviceIdType.MESH
BF16, F32, I32 = jnp.bfloat16, jnp.float32, jnp.int32
RING, SIDE = 4, 64
BLOCKS, SHARDS, EDGE, HID = 12, 8, 128, 256
CHUNK = 192
REPS = 8
NONE = BLOCKS
EMPTY = 192
ROOT = math.sqrt(2.0 / math.pi)
CUBIC = 0.044715


def wrap(value, size):
    return lax.rem(value, size)


def turned(part, x, y, z):
    at = (x, y, z)
    return at[(part + 2) % 3], at[(part + 1) % 3], at[part]


def place(part, x, y, z):
    c, b, a = turned(part, x, y, z)
    return part * 64 + c * 16 + b * 4 + a


def kernel(scale, feat, weight_in, bias_in, tiles, cols_in, degree_in, grad_in,
           act_out, fgrad_out, wgrad_out, bgrad_out,
           weight, bias, cols, degree, grad, act, fgrad,
           swapped, flipped, table_own, table_in, table, gathered,
           theirs, arrived, mine, shares, landed, spread,
           chain_own, chain, grads, land_r, land_y, land_row, land_piece,
           wterm, wx, wcore_out, wcore, whi_out, whi, wrep, wall, bsum_out,
           sems):
    dom, rep = lax.axis_index("dom"), lax.axis_index("rep")
    core = wrap(dom, 2)
    x = wrap(lax.div(dom, 2), 4)
    y_hi = lax.div(dom, 8)
    z, y_lo = lax.div(rep, 2), wrap(rep, 2)
    y = y_hi * 2 + y_lo
    at = (x, y, z)

    def near(axis, step):
        to = list(at)
        to[axis] = wrap(at[axis] + step, RING)
        return (lax.div(to[1], 2) * 4 + to[0]) * 2 + core, to[2] * 2 + wrap(to[1], 2)

    def peer(k):
        return dom, wrap(rep + k, REPS)

    partner = (dom + 1 - 2 * core, rep)
    across = (wrap(dom + 8, 16), rep)

    barrier = pltpu.get_barrier_semaphore()

    def greet(target):
        pl.semaphore_signal(barrier, inc=1, device_id=target, device_id_type=MESH)

    for axis in range(3):
        for step in (1, 3, 2):
            greet(near(axis, step))
    greet(partner)
    for k in range(1, REPS):
        greet(peer(k))

    used = [0]
    started = []

    def lane(count=1):
        used[0] += count
        return used[0] - count

    def local(src, dst):
        copy = pltpu.make_async_copy(src, dst, sems.at[lane()])
        copy.start()
        return copy

    def remote(src, dst, target, slot=None):
        slot = lane(2) if slot is None else slot
        return pltpu.make_async_remote_copy(
            src_ref=src, dst_ref=dst, send_sem=sems.at[slot], recv_sem=sems.at[slot + 1],
            device_id=target, device_id_type=MESH)

    def send(src, dst, target, slot=None):
        copy = remote(src, dst, target, slot)
        copy.start()
        started.append(copy)
        return copy

    small = [local(cols_in, cols), local(degree_in, degree)]
    pieces = [local(feat.at[pl.ds(part * SIDE, SIDE)], gathered.at[place(part, x, y, z)]) for part in range(3)]
    own_tiles = local(tiles.at[:, core], swapped.at[0])
    dense_in = [local(weight_in, weight), local(bias_in, bias), local(grad_in, grad)]
    gathered[EMPTY] = jnp.zeros((SIDE, HID), BF16)

    pl.semaphore_wait(barrier, 9 + 1 + REPS - 1)

    def row_of(part, c, b):
        return gathered.at[pl.ds(part * 64 + c * 16 + b * 4, 4)]

    def half_of(part, b, h):
        return gathered.at[pl.ds(part * 64 + at[(part + 2) % 3] * 16 + b * 4 + 2 * h, 2)]

    first = []
    for part in range(3):
        for step in (1, 3, 2):
            first.append(send(feat.at[pl.ds(part * SIDE, SIDE)], gathered.at[place(part, x, y, z)], near(part, step)))
    tile_copy = send(tiles.at[:, 1 - core], swapped.at[1], partner)

    def flip(which, b0, count):
        def body(b, carry):
            for s in range(SHARDS):
                spot = (s % 4) * 2 + s // 4
                flipped[which, b, pl.ds(spot * EDGE, EDGE), :] = jnp.transpose(swapped[which, b * SHARDS + s])
            return carry
        lax.fori_loop(b0, b0 + count, body, 0)

    for copy in pieces:
        copy.wait()
    for copy in first:
        copy.wait_recv()

    slots_1 = [[[lane(2) for k in range(3)] for way in range(2)] for part in range(3)]
    slots_2 = [[[lane(2) for k in range(6)] for way in range(2)] for part in range(3)]
    FIRST, SECOND = (0, 1), (3, 2)

    def ways():
        for part in range(3):
            for way in range(2):
                yield part, way, (1 if way == 0 else 3)

    def round_1(part, way, step, k, go):
        m = at[(part + 1) % 3]
        h = way if k in (0, 2) else 1 - way
        if go:
            b = m if k < 2 else wrap(m + 4 - step, RING)
        else:
            b = wrap(m + (4 - step) * (1 if k < 2 else 2), RING)
        ref = half_of(part, b, h)
        target, slot = near((part + 1) % 3, step), slots_1[part][way][k]
        if go:
            send(ref, ref, target, slot)
        else:
            remote(ref, ref, target, slot).wait_recv()

    def round_2(part, way, step, k, go):
        m, b0 = at[(part + 2) % 3], at[(part + 1) % 3]
        offset = k if k < 4 else (FIRST if way == 0 else SECOND)[k - 4]
        if go:
            c = m if k < 4 else wrap(m + 4 - step, RING)
        else:
            c = wrap(m + (4 - step) * (1 if k < 4 else 2), RING)
        ref = row_of(part, c, wrap(b0 + offset, RING))
        target, slot = near((part + 2) % 3, step), slots_2[part][way][k]
        if go:
            send(ref, ref, target, slot)
        else:
            remote(ref, ref, target, slot).wait_recv()

    def each(action, k, go):
        for part, way, step in ways():
            action(part, way, step, k, go)

    each(round_1, 0, True)
    each(round_1, 1, True)
    each(round_2, 0, True)

    for copy in small:
        copy.wait()
    col = cols[:, 0, :]
    live = rep < degree[...]
    shard = lax.div(lax.broadcasted_iota(I32, (BLOCKS, 16), 1), 2)
    shard_x, shard_y = wrap(shard, 4), lax.div(shard, 4) * 2
    block = lax.broadcasted_iota(I32, (BLOCKS, 16), 0)
    table_own[...] = jnp.zeros(table_own.shape, I32)
    for h in range(2):
        q = 2 * col + h
        r = (q * 11) >> 5
        part, to_z = q - 3 * r, r >> 1
        to_y = shard_y + (r - 2 * to_z)
        spot = jnp.where(part == 0, place(0, shard_x, to_y, to_z),
                         jnp.where(part == 1, place(1, shard_x, to_y, to_z), place(2, shard_x, to_y, to_z)))
        table_own[16 * h:16 * h + BLOCKS, 0:16] = jnp.where(live, spot, EMPTY)
    third = (block * 11) >> 5
    turn_of = wrap(third + 4 - z, RING)
    rank = jnp.where(turn_of == 0, 0, jnp.where(turn_of == 3, 3, jnp.where(turn_of == 1, 6, 9))) + block - 3 * third
    before = jnp.full((BLOCKS, 16), -1, I32)
    last = jnp.full((BLOCKS, 16), -1, I32)
    for b in range(BLOCKS):
        here, spot = live[b:b + 1], rank[b:b + 1]
        before = jnp.where((col == col[b:b + 1]) & here & (spot < rank), jnp.maximum(before, spot), before)
        last = jnp.where((block == col[b:b + 1]) & here, jnp.maximum(last, spot), last)
    table_own[32:32 + BLOCKS, 0:16] = jnp.where(before < 0, NONE, before)
    table_own[48:48 + BLOCKS, 0:16] = jnp.where(last < 0, NONE, last)
    table_copy = send(table_own, table_in, partner)
    own_table = local(table_own, table.at[0])

    own_tiles.wait()
    flip(0, 0, 1)
    each(round_1, 0, False)
    each(round_1, 2, True)
    each(round_1, 1, False)
    each(round_2, 1, True)
    each(round_2, 3, True)
    flip(0, 1, 1)
    each(round_2, 0, False)
    for part, way, step in ways():
        if way == 0:
            round_2(part, way, step, 4, True)
    each(round_1, 2, False)
    each(round_2, 2, True)
    flip(0, 2, 4)
    each(round_2, 1, False)
    each(round_2, 3, False)
    for part, way, step in ways():
        if way == 0:
            round_2(part, way, step, 5, True)
        else:
            round_2(part, way, step, 4, True)
    flip(0, 6, 6)
    own_table.wait()
    table_copy.wait_recv()
    their_table = local(table_in, table.at[1])
    tile_copy.wait_recv()
    each(round_2, 2, False)
    for part, way, step in ways():
        if way == 1:
            round_2(part, way, step, 5, True)
    flip(1, 0, 12)
    their_table.wait()
    each(round_2, 4, False)
    each(round_2, 5, False)

    def entry(which, kind, b, s):
        return table[which, kind * 16 + b, 2 * s + core]

    def row_block(which, b):
        lhs = jnp.concatenate([swapped[which, b * SHARDS + s] for s in range(SHARDS)], axis=1)
        rhs = jnp.concatenate([gathered[entry(which, h, b, s)] for s in range(SHARDS) for h in range(2)], axis=0)
        return jnp.dot(lhs, rhs, preferred_element_type=F32)

    def rows_of(r):
        return pl.ds(pl.multiple_of(r * CHUNK, CHUNK), CHUNK)

    def edge_of(b):
        return pl.ds(pl.multiple_of(b * EDGE, EDGE), EDGE)

    def their_block(b, carry):
        theirs[edge_of(b), :] = row_block(1, b).astype(BF16)
        return carry

    def my_block(b, carry):
        mine[edge_of(b), :] = row_block(0, b)
        return carry

    def beside(dz, dy):
        return wrap(z + dz, RING) * 2 + wrap(y_lo + dy, 2)

    def share(dz, dy):
        to = beside(dz, dy)
        rows = rows_of(to)
        shares[to] = (mine[rows, :] + arrived[rows, :].astype(F32)).astype(BF16)
        return send(shares.at[to], landed.at[rep], (dom, to))

    swap, slots = [], []
    order = (2, 1, 3, 0)
    for g in range(4):
        base = wrap(z + order[g], RING)
        lax.fori_loop(base * 3, base * 3 + 3, their_block, 0)
        rows = pl.ds(pl.multiple_of(base * 384, 384), 384)
        swap.append(send(theirs.at[rows], arrived.at[rows], partner))
        if g:
            swap[g - 1].wait_recv()
            for dy in (1, 0):
                slots.append((order[g - 1], dy, share(order[g - 1], dy)))
        lax.fori_loop(base * 3, base * 3 + 3, my_block, 0)
    swap[3].wait_recv()
    slots.append((0, 1, share(0, 1)))

    total = mine[rows_of(rep), :] + arrived[rows_of(rep), :].astype(F32)
    for copy in dense_in:
        copy.wait()
    for dz, dy, copy in slots:
        copy.wait_recv()
        total = total + landed[beside(4 - dz, dy)].astype(F32)

    aggregated = total.astype(BF16)
    v = jnp.dot(aggregated, weight[...], preferred_element_type=F32) + bias[...]
    t = jnp.tanh(ROOT * (v + CUBIC * (v * v * v)))
    slope = 0.5 * (1.0 + t) + 0.5 * v * ((1.0 - t) * (1.0 + t)) * (ROOT * (1.0 + 3.0 * CUBIC * (v * v)))
    delta = (grad[...].astype(F32) * slope).astype(BF16)
    spread[0, rows_of(rep), :] = lax.dot_general(
        delta, weight[...], (((1,), (1,)), ((), ())), preferred_element_type=F32).astype(BF16)
    here = spread.at[0, rows_of(rep)]
    spread_in = {}
    for dz in (0, 1, 3, 2):
        for dy in (0, 1):
            if dz or dy:
                spread_in[dz, dy] = send(here, here, (dom, beside(dz, dy)))
    forward_in = [send(here, spread.at[1, rows_of(rep)], partner)]
    act[...] = (0.5 * v * (1.0 + t)).astype(BF16)
    outgoing = [local(act, act_out)]

    wsum = lax.dot_general(aggregated, delta, (((0,), (0,)), ((), ())), preferred_element_type=F32)
    bsum = jnp.sum(delta.astype(F32).reshape(CHUNK // 8, 8, HID), axis=0)
    for k in range(RING):
        wterm[k, 0:64, :] = wsum[k * 64:(k + 1) * 64, :]
        wterm[k, 64:72, :] = bsum
    wx[x] = wterm[x]
    w_x = [send(wterm.at[wrap(x + k, RING)], wx.at[x], near(0, k)) for k in range(1, RING)]

    for s in range(SHARDS):
        chain_own[s, NONE] = jnp.zeros((EDGE, HID), F32)
    for s in range(2):
        chain[s, NONE] = jnp.zeros((EDGE, HID), F32)

    for turn_at in range(4):
        dz = (0, 1, 3, 2)[turn_at]
        for dy in (0, 1):
            if dz or dy:
                spread_in[dz, dy].wait_recv()
                rows = rows_of(beside(4 - dz, dy))
                forward_in.append(send(spread.at[0, rows], spread.at[1, rows], partner))
        base = wrap(z + 4 - dz, RING) * 3

        def own_block(j, carry):
            b = base + j
            source = spread[0, edge_of(b), :]
            for to_x in range(4):
                product = jnp.dot(flipped[0, b, pl.ds(to_x * 2 * EDGE, 2 * EDGE), :], source, preferred_element_type=F32)
                for s in range(2):
                    prior = chain_own[to_x * 2 + s, entry(0, 2, b, s * 4 + to_x)]
                    chain_own[to_x * 2 + s, turn_at * 3 + j] = product[s * EDGE:(s + 1) * EDGE] + prior
            return carry
        lax.fori_loop(0, 3, own_block, 0)

    def link(to_x):
        rows = pl.ds(pl.multiple_of(to_x * 2 * EDGE, 2 * EDGE), 2 * EDGE)
        for turn_at in range(4):
            base = wrap(z + (0, 3, 1, 2)[turn_at], RING) * 3
            blocks = [base + j for j in range(3)]
            products = [
                jnp.dot(flipped[1, b, rows, :], spread[1, edge_of(b), :], preferred_element_type=F32) for b in blocks]
            for j, b in enumerate(blocks):
                for s in range(2):
                    prior = chain[s, entry(1, 2, b, s * 4 + to_x)]
                    chain[s, turn_at * 3 + j] = products[j][s * EDGE:(s + 1) * EDGE] + prior

    def close(to_x):
        for s in range(2):
            for c in range(BLOCKS):
                both = (chain_own[to_x * 2 + s, entry(0, 3, c, s * 4 + to_x)]
                        + chain[s, entry(1, 3, c, s * 4 + to_x)]).astype(BF16)
                for h in range(2):
                    q = 2 * c + h
                    part, r = q % 3, q // 3
                    grads[(part,) + turned(part, to_x, s * 2 + r % 2, r // 2)] = both[h * SIDE:(h + 1) * SIDE]

    off = (2, 1, 3, 0)
    to_xs = [wrap(x + d, RING) for d in off]
    to_zs = [wrap(z + d, RING) for d in off]
    slots_r = [[[[lane(2) for k in range(3)] for way in range(2)] for g in range(4)] for part in range(3)]
    ring_of = (2, 0, 1)

    def quarter(part, plane, g, h):
        if part == 0:
            return grads.at[0, plane, pl.ds(2 * h, 2), to_xs[g]]
        return grads.at[part, plane, (to_zs if part == 1 else to_xs)[g], pl.ds(2 * h, 2)]

    def land_of(part, g, way, k):
        return land_r.at[((part * 4 + g) * 2 + way) * 3 + k]

    def quarter_copy(part, g, way, k):
        axis, step = ring_of[part], (1, 3)[way]
        plane = wrap(at[axis] + (2 if k == 0 else step), RING)
        h = way if k in (0, 2) else 1 - way
        return remote(quarter(part, plane, g, h), land_of(part, g, way, k), near(axis, step), slots_r[part][g][way][k])

    def begin(copy):
        copy.start()
        started.append(copy)

    def begin_each(parts, g, k):
        for part in parts:
            for way in range(2):
                begin(quarter_copy(part, g, way, k))

    def add_to(ref, *others):
        full = ref[...].astype(F32)
        for other in others:
            full = full + other[...].astype(F32)
        ref[...] = full.astype(BF16)

    def pass_on(g):
        for part in range(3):
            for way in range(2):
                quarter_copy(part, g, way, 0).wait_recv()
                plane = wrap(at[ring_of[part]] + (1, 3)[way], RING)
                add_to(quarter(part, plane, g, way), land_of(part, g, way, 0))
                begin(quarter_copy(part, g, way, 2))

    rows_sent = {}

    def settle(g):
        for part in range(3):
            for way in range(2):
                for k in (1, 2):
                    quarter_copy(part, g, way, k).wait_recv()
            plane = at[ring_of[part]]
            for h in range(2):
                add_to(quarter(part, plane, g, h), land_of(part, g, h, 2), land_of(part, g, 1 - h, 1))
            if part == 0:
                for k in range(1, RING):
                    rows_sent[0, g, k] = send(
                        grads.at[0, z, wrap(y + k, RING), to_xs[g]], land_y.at[g * 3 + k - 1], near(1, k))
            elif g < 3:
                row = (to_zs if part == 1 else to_xs)[g]
                rows_sent[part, g] = send(
                    grads.at[part, plane, row], land_row.at[(part - 1) * 3 + g], near((2, 0)[part - 1], off[g]))

    pieces_sent = {}

    def column_in(g):
        for k in range(1, RING):
            rows_sent[0, g, k].wait_recv()
        piece = grads.at[0, z, y, to_xs[g]]
        add_to(piece, *[land_y.at[g * 3 + k] for k in range(3)])
        if g < 3:
            pieces_sent[0, g] = send(piece, land_piece.at[g], near(0, off[g]))

    def row_in(part):
        for g in range(3):
            rows_sent[part, g].wait_recv()
        plane, row = (x, z) if part == 1 else (y, x)
        add_to(grads.at[part, plane, row], *[land_row.at[(part - 1) * 3 + g] for g in range(3)])
        axis = (1, 2)[part - 1]
        for g in range(3):
            pieces_sent[part, g] = send(grads.at[part, plane, row, wrap(at[axis] + off[g], RING)],
                                        land_piece.at[part * 3 + g], near(axis, off[g]))

    def piece_in(part):
        plane, row, spot = turned(part, x, y, z)
        full = grads[part, plane, row, spot].astype(F32)
        for g in range(3):
            pieces_sent[part, g].wait_recv()
            full = full + land_piece[part * 3 + g].astype(F32)
        fgrad[pl.ds(part * SIDE, SIDE), :] = full.astype(BF16)

    for copy in forward_in:
        copy.wait_recv()
    for g in range(4):
        link(to_xs[g])
        close(to_xs[g])
        begin_each((0, 2), g, 0)
        if g == 0:
            for q in range(4):
                begin_each((1,), q, 0)

    for copy in w_x:
        copy.wait_recv()
    wx[0] = wx[0] + wx[1] + wx[2] + wx[3]
    wcore_out[0:32, :] = wx[0, pl.ds(pl.multiple_of((1 - core) * 32, 32), 32), :]
    wcore_out[32:40, :] = wx[0, 64:72, :]
    w_core = send(wcore_out, wcore, partner)

    begin_each(range(3), 0, 1)
    pass_on(0)
    w_core.wait_recv()
    wcore[0:32, :] = wcore[0:32, :] + wx[0, pl.ds(pl.multiple_of(core * 32, 32), 32), :]
    wcore[32:40, :] = wcore[32:40, :] + wx[0, 64:72, :]
    whi_out[0:16, :] = wcore[pl.ds(pl.multiple_of((1 - y_hi) * 16, 16), 16), :]
    whi_out[16:24, :] = wcore[32:40, :]
    w_hi = send(whi_out, whi, across)

    begin_each(range(3), 1, 1)
    pass_on(1)
    w_hi.wait_recv()
    wrep[rep, 0:16, :] = whi[0:16, :] + wcore[pl.ds(pl.multiple_of(y_hi * 16, 16), 16), :]
    wrep[rep, 16:24, :] = whi[16:24, :] + wcore[32:40, :]
    w_rep = [send(wrep.at[rep], wrep.at[rep], peer(k)) for k in range(1, REPS)]

    begin_each(range(3), 2, 1)
    pass_on(2)
    settle(0)
    for copy in w_rep:
        copy.wait_recv()
    wfull = wrep[0]
    for r in range(1, REPS):
        wfull = wfull + wrep[r]
    wfull = wfull * scale
    bsum_out[...] = jnp.sum(wfull[16:24], axis=0, keepdims=True)
    outgoing.append(local(bsum_out, bgrad_out))

    def wrows(start, count):
        return wall.at[pl.ds(pl.multiple_of(start, 16), count)]

    wall[pl.ds(pl.multiple_of(x * 64 + core * 32 + y_hi * 16, 16), 16), :] = wfull[0:16]
    ref = wrows(x * 64 + core * 32 + y_hi * 16, 16)
    w_hi = send(ref, ref, across)

    begin_each(range(3), 3, 1)
    pass_on(3)
    settle(1)
    w_hi.wait_recv()
    ref = wrows(x * 64 + core * 32, 32)
    w_core = send(ref, ref, partner)
    column_in(0)
    settle(2)
    w_core.wait_recv()
    ref = wrows(x * 64, 64)
    w_x = [send(ref, ref, near(0, k)) for k in range(1, RING)]
    column_in(1)
    settle(3)
    row_in(1)
    row_in(2)
    column_in(2)
    for copy in w_x:
        copy.wait_recv()
    outgoing.append(local(wall, wgrad_out))
    column_in(3)
    for part in (0, 1, 2):
        piece_in(part)
    outgoing.append(local(fgrad, fgrad_out))
    for copy in started:
        copy.wait_send()
    for copy in outgoing:
        copy.wait()


def hand_over(*refs):
    ins, outs, held, sems = refs[:4], refs[4:8], refs[8:12], refs[12]
    copies = [pltpu.make_async_copy(ins[k], held[k], sems.at[k]) for k in range(4)]
    for copy in copies:
        copy.start()
    onward = []
    for k in range(4):
        copies[k].wait()
        onward.append(pltpu.make_async_copy(held[k], outs[k], sems.at[4 + k]))
        onward[k].start()
    for copy in onward:
        copy.wait()


def body(features, weight, bias, adj_tiles, adj_cols, degree, grad_out):
    anywhere = pl.BlockSpec(memory_space=pl.ANY)
    rows = BLOCKS * EDGE
    scale = 1.0 / math.sqrt(CHUNK * REPS * 16)
    outs = (
        jax.ShapeDtypeStruct((CHUNK, HID), BF16),
        jax.ShapeDtypeStruct((CHUNK, HID), BF16),
        jax.ShapeDtypeStruct((HID, HID), F32),
        jax.ShapeDtypeStruct((1, HID), F32),
    )
    call = pl.pallas_call(
        lambda *refs: kernel(scale, *refs),
        out_shape=outs,
        in_specs=[anywhere] * 7,
        out_specs=(anywhere,) * 4,
        scratch_shapes=[
            pltpu.VMEM((HID, HID), BF16),
            pltpu.VMEM((1, HID), F32),
            pltpu.VMEM((BLOCKS, 1, 16), I32),
            pltpu.VMEM((BLOCKS, 16), I32),
            pltpu.VMEM((CHUNK, HID), BF16),
            pltpu.VMEM((CHUNK, HID), BF16),
            pltpu.VMEM((CHUNK, HID), BF16),
            pltpu.VMEM((2, BLOCKS * SHARDS, EDGE, EDGE), BF16),
            pltpu.VMEM((2, BLOCKS, SHARDS * EDGE, EDGE), BF16),
            pltpu.VMEM((64, 128), I32),
            pltpu.VMEM((64, 128), I32),
            pltpu.SMEM((2, 64, 128), I32),
            pltpu.VMEM((193, SIDE, HID), BF16),
            pltpu.VMEM((rows, HID), BF16),
            pltpu.VMEM((rows, HID), BF16),
            pltpu.VMEM((rows, HID), F32),
            pltpu.VMEM((REPS, CHUNK, HID), BF16),
            pltpu.VMEM((REPS, CHUNK, HID), BF16),
            pltpu.VMEM((2, rows, HID), BF16),
            pltpu.VMEM((SHARDS, 13, EDGE, HID), F32),
            pltpu.VMEM((2, 13, EDGE, HID), F32),
            pltpu.VMEM((3, 4, 4, 4, SIDE, HID), BF16),
            pltpu.VMEM((72, 2, SIDE, HID), BF16),
            pltpu.VMEM((12, SIDE, HID), BF16),
            pltpu.VMEM((6, 4, SIDE, HID), BF16),
            pltpu.VMEM((9, SIDE, HID), BF16),
            pltpu.VMEM((RING, 72, HID), F32),
            pltpu.VMEM((RING, 72, HID), F32),
            pltpu.VMEM((40, HID), F32),
            pltpu.VMEM((40, HID), F32),
            pltpu.VMEM((24, HID), F32),
            pltpu.VMEM((24, HID), F32),
            pltpu.VMEM((REPS, 24, HID), F32),
            pltpu.VMEM((HID, HID), F32),
            pltpu.VMEM((1, HID), F32),
            pltpu.SemaphoreType.DMA((512,)),
        ],
        compiler_params=pltpu.CompilerParams(
            collective_id=0, has_side_effects=True, vmem_limit_bytes=61 * 1024 * 1024),
    )
    results = call(
        features, weight, bias.reshape(1, HID),
        adj_tiles.reshape(BLOCKS * SHARDS, 2, EDGE, EDGE), adj_cols.transpose(0, 2, 1), degree, grad_out)
    act, fgrad, wgrad, bgrad = pl.pallas_call(
        hand_over,
        out_shape=outs,
        in_specs=[anywhere] * 4,
        out_specs=(anywhere,) * 4,
        scratch_shapes=[pltpu.VMEM(out.shape, out.dtype) for out in outs] + [pltpu.SemaphoreType.DMA((8,))],
    )(*results)
    return act, fgrad, wgrad, bgrad.reshape(HID)


def solution(mesh):
    return jax.shard_map(
        body,
        mesh=mesh,
        in_specs=(
            P(("dom", "rep"), None),
            P(),
            P(),
            P("dom", None, "rep", None, None),
            P("dom", None, "rep"),
            P("dom", None),
            P(("dom", "rep"), None),
        ),
        out_specs=(P(("dom", "rep"), None), P(("dom", "rep"), None), P(), P()),
        check_vma=False,
    )
```

```python
import math

import jax
import jax.numpy as jnp
from jax import lax
from jax.experimental import pallas as pl
from jax.experimental.pallas import tpu as pltpu
from jax.sharding import PartitionSpec as P

MESH = pl.DeviceIdType.MESH
BF16, F32, I32 = jnp.bfloat16, jnp.float32, jnp.int32
RING, SIDE = 4, 64
BLOCKS, SHARDS, EDGE, HID = 12, 8, 128, 256
CHUNK = 192
REPS = 8
NONE = BLOCKS
EMPTY = 192
ROOT = math.sqrt(2.0 / math.pi)
CUBIC = 0.044715


def wrap(value, size):
    return lax.rem(value, size)


def turned(part, x, y, z):
    at = (x, y, z)
    return at[(part + 2) % 3], at[(part + 1) % 3], at[part]


def place(part, x, y, z):
    c, b, a = turned(part, x, y, z)
    return part * 64 + c * 16 + b * 4 + a


def kernel(scale, feat, weight_in, bias_in, tiles, cols_in, degree_in, grad_in,
           act_out, fgrad_out, wgrad_out, bgrad_out,
           weight, bias, cols, degree, grad, act, fgrad,
           swapped, flipped, table_own, table_in, table, gathered,
           theirs, arrived, mine, shares, landed, spread,
           chain_own, chain, grads, land_r, land_y, land_row, land_piece,
           wterm, wx, wcore_out, wcore, whi_out, whi, wrep, wall, bsum_out,
           sems):
    dom, rep = lax.axis_index("dom"), lax.axis_index("rep")
    core = wrap(dom, 2)
    x = wrap(lax.div(dom, 2), 4)
    y_hi = lax.div(dom, 8)
    z, y_lo = lax.div(rep, 2), wrap(rep, 2)
    y = y_hi * 2 + y_lo
    at = (x, y, z)

    def near(axis, step):
        to = list(at)
        to[axis] = wrap(at[axis] + step, RING)
        return (lax.div(to[1], 2) * 4 + to[0]) * 2 + core, to[2] * 2 + wrap(to[1], 2)

    def peer(k):
        return dom, wrap(rep + k, REPS)

    partner = (dom + 1 - 2 * core, rep)
    across = (wrap(dom + 8, 16), rep)

    barrier = pltpu.get_barrier_semaphore()

    def greet(target):
        pl.semaphore_signal(barrier, inc=1, device_id=target, device_id_type=MESH)

    for axis in range(3):
        for step in (1, 3, 2):
            greet(near(axis, step))
    greet(partner)
    for k in range(1, REPS):
        greet(peer(k))

    used = [0]
    started = []

    def lane(count=1):
        used[0] += count
        return used[0] - count

    def local(src, dst):
        copy = pltpu.make_async_copy(src, dst, sems.at[lane()])
        copy.start()
        return copy

    def remote(src, dst, target, slot=None):
        slot = lane(2) if slot is None else slot
        return pltpu.make_async_remote_copy(
            src_ref=src, dst_ref=dst, send_sem=sems.at[slot], recv_sem=sems.at[slot + 1],
            device_id=target, device_id_type=MESH)

    def send(src, dst, target, slot=None):
        copy = remote(src, dst, target, slot)
        copy.start()
        started.append(copy)
        return copy

    small = [local(cols_in, cols), local(degree_in, degree)]
    pieces = [local(feat.at[pl.ds(part * SIDE, SIDE)], gathered.at[place(part, x, y, z)]) for part in range(3)]
    own_tiles = local(tiles.at[:, core], swapped.at[0])
    dense_in = [local(weight_in, weight), local(bias_in, bias), local(grad_in, grad)]
    gathered[EMPTY] = jnp.zeros((SIDE, HID), BF16)

    pl.semaphore_wait(barrier, 9 + 1 + REPS - 1)

    def piece_of(part, c, b, a):
        return gathered.at[part * 64 + c * 16 + b * 4 + a]

    def move(part, axis, way, ref, slot, go):
        copy = remote(ref, ref, near(axis, (1, 3)[way]), slot)
        if go:
            copy.start()
            started.append(copy)
        else:
            copy.wait_recv()

    def from_where(m, way, passed, go):
        return wrap(m + (passed + (0 if go else 1)) * (4 - (1, 3)[way]), RING)

    slots_1 = [[[lane(2) for k in range(8)] for way in range(2)] for part in range(3)]
    slots_2 = [[[lane(2) for k in range(12)] for way in range(2)] for part in range(3)]

    def round_1(way, o, passed, go, parts=(0, 1, 2)):
        for part in parts:
            b = from_where(at[(part + 1) % 3], way, passed, go)
            ref = piece_of(part, at[(part + 2) % 3], b, wrap(at[part] + o, RING))
            move(part, (part + 1) % 3, way, ref, slots_1[part][way][4 * passed + o], go)

    def round_2(way, o, go, parts=(0, 1, 2)):
        for part in parts:
            c = from_where(at[(part + 2) % 3], way, 0, go)
            ref = piece_of(part, c, at[(part + 1) % 3], wrap(at[part] + o, RING))
            move(part, (part + 2) % 3, way, ref, slots_2[part][way][o], go)

    def round_3(way, row, passed, go):
        for part in range(3):
            c = from_where(at[(part + 2) % 3], way, passed, go)
            b = wrap(at[(part + 1) % 3] + row, RING)
            ref = gathered.at[pl.ds(part * 64 + c * 16 + b * 4, 4)]
            move(part, (part + 2) % 3, way, ref, slots_2[part][way][4 + 4 * passed + row], go)

    for copy in pieces:
        copy.wait()
    first = {}
    for part in range(3):
        own = gathered.at[place(part, x, y, z)]
        for o in (3, 1, 2):
            first[part, o] = send(own, own, near(part, 4 - o))
    for way in range(2):
        round_1(way, 0, 0, True)
        round_2(way, 0, True)
    tile_copy = send(tiles.at[:, 1 - core], swapped.at[1], partner)

    def flip(which, b0, count):
        def body(b, carry):
            for s in range(SHARDS):
                spot = (s % 4) * 2 + s // 4
                flipped[which, b, pl.ds(spot * EDGE, EDGE), :] = jnp.transpose(swapped[which, b * SHARDS + s])
            return carry
        lax.fori_loop(b0, b0 + count, body, 0)

    for copy in small:
        copy.wait()
    col = cols[:, 0, :]
    live = rep < degree[...]
    shard = lax.div(lax.broadcasted_iota(I32, (BLOCKS, 16), 1), 2)
    shard_x, shard_y = wrap(shard, 4), lax.div(shard, 4) * 2
    block = lax.broadcasted_iota(I32, (BLOCKS, 16), 0)
    table_own[...] = jnp.zeros(table_own.shape, I32)
    for h in range(2):
        q = 2 * col + h
        r = (q * 11) >> 5
        part, to_z = q - 3 * r, r >> 1
        to_y = shard_y + (r - 2 * to_z)
        spot = jnp.where(part == 0, place(0, shard_x, to_y, to_z),
                         jnp.where(part == 1, place(1, shard_x, to_y, to_z), place(2, shard_x, to_y, to_z)))
        table_own[16 * h:16 * h + BLOCKS, 0:16] = jnp.where(live, spot, EMPTY)
    third = (block * 11) >> 5
    turn_of = wrap(third + 4 - z, RING)
    rank = jnp.where(turn_of == 0, 0, jnp.where(turn_of == 3, 3, jnp.where(turn_of == 1, 6, 9))) + block - 3 * third
    before = jnp.full((BLOCKS, 16), -1, I32)
    last = jnp.full((BLOCKS, 16), -1, I32)
    for b in range(BLOCKS):
        here, spot = live[b:b + 1], rank[b:b + 1]
        before = jnp.where((col == col[b:b + 1]) & here & (spot < rank), jnp.maximum(before, spot), before)
        last = jnp.where((block == col[b:b + 1]) & here, jnp.maximum(last, spot), last)
    table_own[32:32 + BLOCKS, 0:16] = jnp.where(before < 0, NONE, before)
    table_own[48:48 + BLOCKS, 0:16] = jnp.where(last < 0, NONE, last)
    table_copy = send(table_own, table_in, partner)
    own_table = local(table_own, table.at[0])

    for o in (3, 1, 2):
        for part in range(3):
            first[part, o].wait_recv()
            for way in range(2):
                round_1(way, o, 0, True, (part,))
                round_2(way, o, True, (part,))
    round_1(0, 0, 0, False)
    round_1(0, 0, 1, True)
    round_1(1, 0, 0, False)
    own_tiles.wait()
    flip(0, 0, 1)
    round_1(1, 3, 0, False)
    round_1(1, 3, 1, True)
    round_1(0, 3, 0, False)
    round_1(0, 1, 0, False)
    round_1(0, 1, 1, True)
    round_1(1, 1, 0, False)
    round_1(1, 2, 0, False)
    round_1(1, 2, 1, True)
    round_1(0, 2, 0, False)
    round_3(0, 1, 0, True)
    round_3(1, 3, 0, True)
    round_3(0, 3, 0, True)
    for o in range(4):
        for way in range(2):
            round_2(way, o, False)
    round_3(0, 0, 1, True)
    for o in (0, 1):
        round_1(0, o, 1, False)
    for o in (3, 2):
        round_1(1, o, 1, False)
    round_3(1, 2, 0, True)
    round_3(1, 1, 0, True)
    round_3(0, 2, 0, True)
    flip(0, 1, 5)
    round_3(0, 1, 0, False)
    round_3(0, 1, 1, True)
    round_3(1, 3, 0, False)
    round_3(1, 3, 1, True)
    flip(0, 6, 4)
    round_3(1, 2, 0, False)
    round_3(1, 2, 1, True)
    flip(0, 10, 2)
    own_table.wait()
    table_copy.wait_recv()
    their_table = local(table_in, table.at[1])
    tile_copy.wait_recv()
    flip(1, 0, 12)
    their_table.wait()
    for way, rows in ((0, (3, 2)), (1, (1,))):
        for row in rows:
            round_3(way, row, 0, False)
    for way, rows in ((0, (0, 1)), (1, (3, 2))):
        for row in rows:
            round_3(way, row, 1, False)

    def entry(which, kind, b, s):
        return table[which, kind * 16 + b, 2 * s + core]

    def row_block(which, b):
        lhs = jnp.concatenate([swapped[which, b * SHARDS + s] for s in range(SHARDS)], axis=1)
        rhs = jnp.concatenate([gathered[entry(which, h, b, s)] for s in range(SHARDS) for h in range(2)], axis=0)
        return jnp.dot(lhs, rhs, preferred_element_type=F32)

    def rows_of(r):
        return pl.ds(pl.multiple_of(r * CHUNK, CHUNK), CHUNK)

    def edge_of(b):
        return pl.ds(pl.multiple_of(b * EDGE, EDGE), EDGE)

    def their_block(b, carry):
        theirs[edge_of(b), :] = row_block(1, b).astype(BF16)
        return carry

    def my_block(b, carry):
        mine[edge_of(b), :] = row_block(0, b)
        return carry

    def beside(dz, dy):
        return wrap(z + dz, RING) * 2 + wrap(y_lo + dy, 2)

    def share(dz, dy):
        to = beside(dz, dy)
        rows = rows_of(to)
        shares[to] = (mine[rows, :] + arrived[rows, :].astype(F32)).astype(BF16)
        return send(shares.at[to], landed.at[rep], (dom, to))

    swap, slots = [], []
    order = (2, 1, 3, 0)
    for g in range(4):
        base = wrap(z + order[g], RING)
        lax.fori_loop(base * 3, base * 3 + 3, their_block, 0)
        rows = pl.ds(pl.multiple_of(base * 384, 384), 384)
        swap.append(send(theirs.at[rows], arrived.at[rows], partner))
        if g:
            swap[g - 1].wait_recv()
            for dy in (1, 0):
                slots.append((order[g - 1], dy, share(order[g - 1], dy)))
        lax.fori_loop(base * 3, base * 3 + 3, my_block, 0)
    swap[3].wait_recv()
    earlier = started[:-5]
    del started[:-5]
    slots.append((0, 1, share(0, 1)))
    for copy in earlier:
        copy.wait_send()

    total = mine[rows_of(rep), :] + arrived[rows_of(rep), :].astype(F32)
    for copy in dense_in:
        copy.wait()
    for dz, dy, copy in slots:
        copy.wait_recv()
        total = total + landed[beside(4 - dz, dy)].astype(F32)

    aggregated = total.astype(BF16)
    v = jnp.dot(aggregated, weight[...], preferred_element_type=F32) + bias[...]
    t = jnp.tanh(ROOT * (v + CUBIC * (v * v * v)))
    slope = 0.5 * (1.0 + t) + 0.5 * v * ((1.0 - t) * (1.0 + t)) * (ROOT * (1.0 + 3.0 * CUBIC * (v * v)))
    delta = (grad[...].astype(F32) * slope).astype(BF16)
    spread[0, rows_of(rep), :] = lax.dot_general(
        delta, weight[...], (((1,), (1,)), ((), ())), preferred_element_type=F32).astype(BF16)
    here = spread.at[0, rows_of(rep)]
    spread_in = {}
    for dz in (0, 1, 3, 2):
        for dy in (0, 1):
            if dz or dy:
                spread_in[dz, dy] = send(here, here, (dom, beside(dz, dy)))
    forward_in = [send(here, spread.at[1, rows_of(rep)], partner)]
    act[...] = (0.5 * v * (1.0 + t)).astype(BF16)
    outgoing = [local(act, act_out)]

    wsum = lax.dot_general(aggregated, delta, (((0,), (0,)), ((), ())), preferred_element_type=F32)
    bsum = jnp.sum(delta.astype(F32).reshape(CHUNK // 8, 8, HID), axis=0)
    for k in range(RING):
        wterm[k, 0:64, :] = wsum[k * 64:(k + 1) * 64, :]
        wterm[k, 64:72, :] = bsum
    wx[x] = wterm[x]
    w_x = [send(wterm.at[wrap(x + k, RING)], wx.at[x], near(0, k)) for k in range(1, RING)]

    for s in range(SHARDS):
        chain_own[s, NONE] = jnp.zeros((EDGE, HID), F32)
    for s in range(2):
        chain[s, NONE] = jnp.zeros((EDGE, HID), F32)

    for turn_at in range(4):
        dz = (0, 1, 3, 2)[turn_at]
        for dy in (0, 1):
            if dz or dy:
                spread_in[dz, dy].wait_recv()
                rows = rows_of(beside(4 - dz, dy))
                forward_in.append(send(spread.at[0, rows], spread.at[1, rows], partner))
        base = wrap(z + 4 - dz, RING) * 3

        def own_block(j, carry):
            b = base + j
            source = spread[0, edge_of(b), :]
            for to_x in range(4):
                product = jnp.dot(flipped[0, b, pl.ds(to_x * 2 * EDGE, 2 * EDGE), :], source, preferred_element_type=F32)
                for s in range(2):
                    prior = chain_own[to_x * 2 + s, entry(0, 2, b, s * 4 + to_x)]
                    chain_own[to_x * 2 + s, turn_at * 3 + j] = product[s * EDGE:(s + 1) * EDGE] + prior
            return carry
        lax.fori_loop(0, 3, own_block, 0)
        if turn_at == 1:
            for copy in w_x:
                copy.wait_recv()
            wx[0] = wx[0] + wx[1] + wx[2] + wx[3]
            wcore_out[0:32, :] = wx[0, pl.ds(pl.multiple_of((1 - core) * 32, 32), 32), :]
            wcore_out[32:40, :] = wx[0, 64:72, :]
            w_core = send(wcore_out, wcore, partner)
        elif turn_at == 3:
            w_core.wait_recv()
            wcore[0:32, :] = wcore[0:32, :] + wx[0, pl.ds(pl.multiple_of(core * 32, 32), 32), :]
            wcore[32:40, :] = wcore[32:40, :] + wx[0, 64:72, :]
            whi_out[0:16, :] = wcore[pl.ds(pl.multiple_of((1 - y_hi) * 16, 16), 16), :]
            whi_out[16:24, :] = wcore[32:40, :]
            w_hi = send(whi_out, whi, across)

    def link(to_x):
        rows = pl.ds(pl.multiple_of(to_x * 2 * EDGE, 2 * EDGE), 2 * EDGE)
        for turn_at in range(4):
            base = wrap(z + (0, 3, 1, 2)[turn_at], RING) * 3
            blocks = [base + j for j in range(3)]
            products = [
                jnp.dot(flipped[1, b, rows, :], spread[1, edge_of(b), :], preferred_element_type=F32) for b in blocks]
            for j, b in enumerate(blocks):
                for s in range(2):
                    prior = chain[s, entry(1, 2, b, s * 4 + to_x)]
                    chain[s, turn_at * 3 + j] = products[j][s * EDGE:(s + 1) * EDGE] + prior

    def close(to_x):
        for s in range(2):
            for c in range(BLOCKS):
                both = (chain_own[to_x * 2 + s, entry(0, 3, c, s * 4 + to_x)]
                        + chain[s, entry(1, 3, c, s * 4 + to_x)]).astype(BF16)
                for h in range(2):
                    q = 2 * c + h
                    part, r = q % 3, q // 3
                    grads[(part,) + turned(part, to_x, s * 2 + r % 2, r // 2)] = both[h * SIDE:(h + 1) * SIDE]

    off = (2, 1, 3, 0)
    to_xs = [wrap(x + d, RING) for d in off]
    to_zs = [wrap(z + d, RING) for d in off]
    slots_r = [[[[lane(2) for k in range(3)] for way in range(2)] for g in range(4)] for part in range(3)]
    ring_of = (2, 0, 1)

    def quarter(part, plane, g, h):
        if part == 0:
            return grads.at[0, plane, pl.ds(2 * h, 2), to_xs[g]]
        return grads.at[part, plane, (to_zs if part == 1 else to_xs)[g], pl.ds(2 * h, 2)]

    def land_of(part, g, way, k):
        return land_r.at[((part * 4 + g) * 2 + way) * 3 + k]

    def quarter_copy(part, g, way, k):
        axis, step = ring_of[part], (1, 3)[way]
        plane = wrap(at[axis] + (2 if k == 0 else step), RING)
        h = way if k in (0, 2) else 1 - way
        return remote(quarter(part, plane, g, h), land_of(part, g, way, k), near(axis, step), slots_r[part][g][way][k])

    def begin(copy):
        copy.start()
        started.append(copy)

    def begin_each(parts, g, k):
        for part in parts:
            for way in range(2):
                begin(quarter_copy(part, g, way, k))

    def add_to(ref, *others):
        full = ref[...].astype(F32)
        for other in others:
            full = full + other[...].astype(F32)
        ref[...] = full.astype(BF16)

    def pass_on(g):
        for part in range(3):
            for way in range(2):
                quarter_copy(part, g, way, 0).wait_recv()
                plane = wrap(at[ring_of[part]] + (1, 3)[way], RING)
                add_to(quarter(part, plane, g, way), land_of(part, g, way, 0))
                begin(quarter_copy(part, g, way, 2))

    rows_sent = {}

    def settle(g):
        for part in range(3):
            for way in range(2):
                for k in (1, 2):
                    quarter_copy(part, g, way, k).wait_recv()
            plane = at[ring_of[part]]
            for h in range(2):
                add_to(quarter(part, plane, g, h), land_of(part, g, h, 2), land_of(part, g, 1 - h, 1))
            if part == 0:
                for k in range(1, RING):
                    rows_sent[0, g, k] = send(
                        grads.at[0, z, wrap(y + k, RING), to_xs[g]], land_y.at[g * 3 + k - 1], near(1, k))
            elif g == 0:
                row, axis = (to_zs, to_xs)[part - 1][0], (2, 0)[part - 1]
                for h in range(2):
                    rows_sent[part, 0, h] = send(grads.at[part, plane, row, pl.ds(2 * h, 2)],
                                                 land_row.at[(part - 1) * 3, pl.ds(2 * h, 2)], near(axis, (1, 3)[h]))
            elif g < 3:
                row = (to_zs, to_xs)[part - 1][g]
                rows_sent[part, 0, g - 1].wait_recv()
                spot = pl.ds(2 * (g - 1), 2)
                add_to(grads.at[part, plane, row, spot], land_row.at[(part - 1) * 3, spot])
                rows_sent[part, g] = send(
                    grads.at[part, plane, row], land_row.at[(part - 1) * 3 + g], near((2, 0)[part - 1], off[g]))

    pieces_sent = {}

    def column_in(g):
        for k in range(1, RING):
            rows_sent[0, g, k].wait_recv()
        piece = grads.at[0, z, y, to_xs[g]]
        add_to(piece, *[land_y.at[g * 3 + k] for k in range(3)])
        if g < 3:
            pieces_sent[0, g] = send(piece, land_piece.at[g], near(0, off[g]))

    def row_in(part):
        for g in (1, 2):
            rows_sent[part, g].wait_recv()
        plane, row = (x, z) if part == 1 else (y, x)
        add_to(grads.at[part, plane, row], *[land_row.at[(part - 1) * 3 + g] for g in (1, 2)])
        axis = (1, 2)[part - 1]
        for g in range(3):
            pieces_sent[part, g] = send(grads.at[part, plane, row, wrap(at[axis] + off[g], RING)],
                                        land_piece.at[part * 3 + g], near(axis, off[g]))

    def piece_in(part):
        plane, row, spot = turned(part, x, y, z)
        full = grads[part, plane, row, spot].astype(F32)
        for g in range(3):
            pieces_sent[part, g].wait_recv()
            full = full + land_piece[part * 3 + g].astype(F32)
        fgrad[pl.ds(part * SIDE, SIDE), :] = full.astype(BF16)

    for copy in forward_in:
        copy.wait_recv()
    for g in range(4):
        link(to_xs[g])
        close(to_xs[g])
        begin_each((0, 2), g, 0)
        if g == 0:
            for q in range(4):
                begin_each((1,), q, 0)

    w_hi.wait_recv()
    wrep[rep, 0:16, :] = whi[0:16, :] + wcore[pl.ds(pl.multiple_of(y_hi * 16, 16), 16), :]
    wrep[rep, 16:24, :] = whi[16:24, :] + wcore[32:40, :]
    w_rep = [send(wrep.at[rep], wrep.at[rep], peer(k)) for k in range(1, REPS)]

    begin_each(range(3), 0, 1)
    pass_on(0)
    begin_each(range(3), 1, 1)
    pass_on(1)
    for copy in w_rep:
        copy.wait_recv()
    wfull = wrep[0]
    for r in range(1, REPS):
        wfull = wfull + wrep[r]
    wfull = wfull * scale
    bsum_out[...] = jnp.sum(wfull[16:24], axis=0, keepdims=True)
    outgoing.append(local(bsum_out, bgrad_out))

    def wrows(start, count):
        return wall.at[pl.ds(pl.multiple_of(start, 16), count)]

    wall[pl.ds(pl.multiple_of(x * 64 + core * 32 + y_hi * 16, 16), 16), :] = wfull[0:16]
    ref = wrows(x * 64 + core * 32 + y_hi * 16, 16)
    w_hi = send(ref, ref, across)

    begin_each(range(3), 2, 1)
    pass_on(2)
    settle(0)
    w_hi.wait_recv()
    ref = wrows(x * 64 + core * 32, 32)
    w_core = send(ref, ref, partner)

    begin_each(range(3), 3, 1)
    pass_on(3)
    settle(1)
    w_core.wait_recv()
    ref = wrows(x * 64, 64)
    w_x = [send(ref, ref, near(0, k)) for k in range(1, RING)]

    column_in(0)
    settle(2)
    column_in(1)
    settle(3)
    row_in(1)
    row_in(2)
    column_in(2)
    for copy in w_x:
        copy.wait_recv()
    outgoing.append(local(wall, wgrad_out))
    column_in(3)
    for part in (0, 1, 2):
        piece_in(part)
    outgoing.append(local(fgrad, fgrad_out))
    for copy in started:
        copy.wait_send()
    for copy in outgoing:
        copy.wait()


def hand_over(*refs):
    ins, outs, held, sems = refs[:4], refs[4:8], refs[8:12], refs[12]
    copies = [pltpu.make_async_copy(ins[k], held[k], sems.at[k]) for k in range(4)]
    for copy in copies:
        copy.start()
    onward = []
    for k in range(4):
        copies[k].wait()
        onward.append(pltpu.make_async_copy(held[k], outs[k], sems.at[4 + k]))
        onward[k].start()
    for copy in onward:
        copy.wait()


def body(features, weight, bias, adj_tiles, adj_cols, degree, grad_out):
    anywhere = pl.BlockSpec(memory_space=pl.ANY)
    rows = BLOCKS * EDGE
    scale = 1.0 / math.sqrt(CHUNK * REPS * 16)
    outs = (
        jax.ShapeDtypeStruct((CHUNK, HID), BF16),
        jax.ShapeDtypeStruct((CHUNK, HID), BF16),
        jax.ShapeDtypeStruct((HID, HID), F32),
        jax.ShapeDtypeStruct((1, HID), F32),
    )
    call = pl.pallas_call(
        lambda *refs: kernel(scale, *refs),
        out_shape=outs,
        in_specs=[anywhere] * 7,
        out_specs=(anywhere,) * 4,
        scratch_shapes=[
            pltpu.VMEM((HID, HID), BF16),
            pltpu.VMEM((1, HID), F32),
            pltpu.VMEM((BLOCKS, 1, 16), I32),
            pltpu.VMEM((BLOCKS, 16), I32),
            pltpu.VMEM((CHUNK, HID), BF16),
            pltpu.VMEM((CHUNK, HID), BF16),
            pltpu.VMEM((CHUNK, HID), BF16),
            pltpu.VMEM((2, BLOCKS * SHARDS, EDGE, EDGE), BF16),
            pltpu.VMEM((2, BLOCKS, SHARDS * EDGE, EDGE), BF16),
            pltpu.VMEM((64, 128), I32),
            pltpu.VMEM((64, 128), I32),
            pltpu.SMEM((2, 64, 128), I32),
            pltpu.VMEM((193, SIDE, HID), BF16),
            pltpu.VMEM((rows, HID), BF16),
            pltpu.VMEM((rows, HID), BF16),
            pltpu.VMEM((rows, HID), F32),
            pltpu.VMEM((REPS, CHUNK, HID), BF16),
            pltpu.VMEM((REPS, CHUNK, HID), BF16),
            pltpu.VMEM((2, rows, HID), BF16),
            pltpu.VMEM((SHARDS, 13, EDGE, HID), F32),
            pltpu.VMEM((2, 13, EDGE, HID), F32),
            pltpu.VMEM((3, 4, 4, 4, SIDE, HID), BF16),
            pltpu.VMEM((72, 2, SIDE, HID), BF16),
            pltpu.VMEM((12, SIDE, HID), BF16),
            pltpu.VMEM((6, 4, SIDE, HID), BF16),
            pltpu.VMEM((9, SIDE, HID), BF16),
            pltpu.VMEM((RING, 72, HID), F32),
            pltpu.VMEM((RING, 72, HID), F32),
            pltpu.VMEM((40, HID), F32),
            pltpu.VMEM((40, HID), F32),
            pltpu.VMEM((24, HID), F32),
            pltpu.VMEM((24, HID), F32),
            pltpu.VMEM((REPS, 24, HID), F32),
            pltpu.VMEM((HID, HID), F32),
            pltpu.VMEM((1, HID), F32),
            pltpu.SemaphoreType.DMA((640,)),
        ],
        compiler_params=pltpu.CompilerParams(
            collective_id=0, has_side_effects=True, vmem_limit_bytes=61 * 1024 * 1024),
    )
    results = call(
        features, weight, bias.reshape(1, HID),
        adj_tiles.reshape(BLOCKS * SHARDS, 2, EDGE, EDGE), adj_cols.transpose(0, 2, 1), degree, grad_out)
    act, fgrad, wgrad, bgrad = pl.pallas_call(
        hand_over,
        out_shape=outs,
        in_specs=[anywhere] * 4,
        out_specs=(anywhere,) * 4,
        scratch_shapes=[pltpu.VMEM(out.shape, out.dtype) for out in outs] + [pltpu.SemaphoreType.DMA((8,))],
    )(*results)
    return act, fgrad, wgrad, bgrad.reshape(HID)


def solution(mesh):
    return jax.shard_map(
        body,
        mesh=mesh,
        in_specs=(
            P(("dom", "rep"), None),
            P(),
            P(),
            P("dom", None, "rep", None, None),
            P("dom", None, "rep"),
            P("dom", None),
            P(("dom", "rep"), None),
        ),
        out_specs=(P(("dom", "rep"), None), P(("dom", "rep"), None), P(), P()),
        check_vma=False,
    )
```

```python
import math

import jax
import jax.numpy as jnp
from jax import lax
from jax.experimental import pallas as pl
from jax.experimental.pallas import tpu as pltpu
from jax.sharding import PartitionSpec as P

MESH = pl.DeviceIdType.MESH
BF16, F32, I32 = jnp.bfloat16, jnp.float32, jnp.int32
RING, SIDE = 4, 64
BLOCKS, SHARDS, EDGE, HID = 12, 8, 128, 256
CHUNK = 192
REPS = 8
NONE = BLOCKS
EMPTY = 192
ROOT = math.sqrt(2.0 / math.pi)
CUBIC = 0.044715


def wrap(value, size):
    return lax.rem(value, size)


def turned(part, x, y, z):
    at = (x, y, z)
    return at[(part + 2) % 3], at[(part + 1) % 3], at[part]


def place(part, x, y, z):
    c, b, a = turned(part, x, y, z)
    return part * 64 + c * 16 + b * 4 + a


def kernel(scale, feat, weight_in, bias_in, tiles, cols_in, degree_in, grad_in,
           act_out, fgrad_out, wgrad_out, bgrad_out,
           weight, bias, cols, degree, grad, act, fgrad,
           swapped, flipped, table_own, table_in, table, gathered,
           theirs, arrived, mine, shares, landed, spread,
           chain_own, chain, grads, land_r, land_y, land_row, land_piece,
           wterm, wx, wcore_out, wcore, whi_out, whi, wrep, wall, bsum_out,
           sems):
    dom, rep = lax.axis_index("dom"), lax.axis_index("rep")
    core = wrap(dom, 2)
    x = wrap(lax.div(dom, 2), 4)
    y_hi = lax.div(dom, 8)
    z, y_lo = lax.div(rep, 2), wrap(rep, 2)
    y = y_hi * 2 + y_lo
    at = (x, y, z)

    def near(axis, step):
        to = list(at)
        to[axis] = wrap(at[axis] + step, RING)
        return (lax.div(to[1], 2) * 4 + to[0]) * 2 + core, to[2] * 2 + wrap(to[1], 2)

    def peer(k):
        return dom, wrap(rep + k, REPS)

    partner = (dom + 1 - 2 * core, rep)
    across = (wrap(dom + 8, 16), rep)

    barrier = pltpu.get_barrier_semaphore()

    def greet(target):
        pl.semaphore_signal(barrier, inc=1, device_id=target, device_id_type=MESH)

    for axis in range(3):
        for step in (1, 3, 2):
            greet(near(axis, step))
    greet(partner)
    for k in range(1, REPS):
        greet(peer(k))

    used = [0]
    started = []

    def lane(count=1):
        used[0] += count
        return used[0] - count

    def local(src, dst):
        copy = pltpu.make_async_copy(src, dst, sems.at[lane()])
        copy.start()
        return copy

    def remote(src, dst, target, slot=None):
        slot = lane(2) if slot is None else slot
        return pltpu.make_async_remote_copy(
            src_ref=src, dst_ref=dst, send_sem=sems.at[slot], recv_sem=sems.at[slot + 1],
            device_id=target, device_id_type=MESH)

    def send(src, dst, target, slot=None):
        copy = remote(src, dst, target, slot)
        copy.start()
        started.append(copy)
        return copy

    small = [local(cols_in, cols), local(degree_in, degree)]
    pieces = [local(feat.at[pl.ds(part * SIDE, SIDE)], gathered.at[place(part, x, y, z)]) for part in range(3)]
    own_tiles = local(tiles.at[:, core], swapped.at[0])
    dense_in = [local(weight_in, weight), local(bias_in, bias), local(grad_in, grad)]
    gathered[EMPTY] = jnp.zeros((SIDE, HID), BF16)

    pl.semaphore_wait(barrier, 9 + 1 + REPS - 1)

    def piece_of(part, c, b, a):
        return gathered.at[part * 64 + c * 16 + b * 4 + a]

    def move(part, axis, way, ref, slot, go):
        copy = remote(ref, ref, near(axis, (1, 3)[way]), slot)
        if go:
            copy.start()
            started.append(copy)
        else:
            copy.wait_recv()

    def from_where(m, way, passed, go):
        return wrap(m + (passed + (0 if go else 1)) * (4 - (1, 3)[way]), RING)

    slots_1 = [[[lane(2) for k in range(8)] for way in range(2)] for part in range(3)]
    slots_2 = [[[lane(2) for k in range(12)] for way in range(2)] for part in range(3)]

    def round_1(way, o, passed, go, parts=(0, 1, 2)):
        for part in parts:
            b = from_where(at[(part + 1) % 3], way, passed, go)
            ref = piece_of(part, at[(part + 2) % 3], b, wrap(at[part] + o, RING))
            move(part, (part + 1) % 3, way, ref, slots_1[part][way][4 * passed + o], go)

    def round_2(way, o, go, parts=(0, 1, 2)):
        for part in parts:
            c = from_where(at[(part + 2) % 3], way, 0, go)
            ref = piece_of(part, c, at[(part + 1) % 3], wrap(at[part] + o, RING))
            move(part, (part + 2) % 3, way, ref, slots_2[part][way][o], go)

    def round_3(way, row, passed, go):
        for part in range(3):
            c = from_where(at[(part + 2) % 3], way, passed, go)
            b = wrap(at[(part + 1) % 3] + row, RING)
            ref = gathered.at[pl.ds(part * 64 + c * 16 + b * 4, 4)]
            move(part, (part + 2) % 3, way, ref, slots_2[part][way][4 + 4 * passed + row], go)

    for copy in pieces:
        copy.wait()
    first = {}
    for part in range(3):
        own = gathered.at[place(part, x, y, z)]
        for o in (3, 1, 2):
            first[part, o] = send(own, own, near(part, 4 - o))
    for way in range(2):
        round_1(way, 0, 0, True)
        round_2(way, 0, True)
    tile_copy = send(tiles.at[:, 1 - core], swapped.at[1], partner)

    def flip(which, b0, count):
        def body(b, carry):
            for s in range(SHARDS):
                spot = (s % 4) * 2 + s // 4
                flipped[which, b, pl.ds(spot * EDGE, EDGE), :] = jnp.transpose(swapped[which, b * SHARDS + s])
            return carry
        lax.fori_loop(b0, b0 + count, body, 0)

    for copy in small:
        copy.wait()
    col = cols[:, 0, :]
    live = rep < degree[...]
    shard = lax.div(lax.broadcasted_iota(I32, (BLOCKS, 16), 1), 2)
    shard_x, shard_y = wrap(shard, 4), lax.div(shard, 4) * 2
    block = lax.broadcasted_iota(I32, (BLOCKS, 16), 0)
    table_own[...] = jnp.zeros(table_own.shape, I32)
    for h in range(2):
        q = 2 * col + h
        r = (q * 11) >> 5
        part, to_z = q - 3 * r, r >> 1
        to_y = shard_y + (r - 2 * to_z)
        spot = jnp.where(part == 0, place(0, shard_x, to_y, to_z),
                         jnp.where(part == 1, place(1, shard_x, to_y, to_z), place(2, shard_x, to_y, to_z)))
        table_own[16 * h:16 * h + BLOCKS, 0:16] = jnp.where(live, spot, EMPTY)
    third = (block * 11) >> 5
    turn_of = wrap(third + 4 - z, RING)
    rank = jnp.where(turn_of == 0, 0, jnp.where(turn_of == 3, 3, jnp.where(turn_of == 1, 6, 9))) + block - 3 * third
    before = jnp.full((BLOCKS, 16), -1, I32)
    last = jnp.full((BLOCKS, 16), -1, I32)
    for b in range(BLOCKS):
        here, spot = live[b:b + 1], rank[b:b + 1]
        before = jnp.where((col == col[b:b + 1]) & here & (spot < rank), jnp.maximum(before, spot), before)
        last = jnp.where((block == col[b:b + 1]) & here, jnp.maximum(last, spot), last)
    table_own[32:32 + BLOCKS, 0:16] = jnp.where(before < 0, NONE, before)
    table_own[48:48 + BLOCKS, 0:16] = jnp.where(last < 0, NONE, last)
    table_copy = send(table_own, table_in, partner)
    own_table = local(table_own, table.at[0])

    for o in (3, 1, 2):
        for part in range(3):
            first[part, o].wait_recv()
            for way in range(2):
                round_1(way, o, 0, True, (part,))
                round_2(way, o, True, (part,))
    round_1(0, 0, 0, False)
    round_1(0, 0, 1, True)
    round_1(1, 0, 0, False)
    own_tiles.wait()
    flip(0, 0, 1)
    round_1(1, 3, 0, False)
    round_1(1, 3, 1, True)
    round_1(0, 3, 0, False)
    round_1(0, 1, 0, False)
    round_1(0, 1, 1, True)
    round_1(1, 1, 0, False)
    round_1(1, 2, 0, False)
    round_1(1, 2, 1, True)
    round_1(0, 2, 0, False)
    round_3(0, 1, 0, True)
    round_3(1, 3, 0, True)
    round_3(0, 3, 0, True)
    for o in range(4):
        for way in range(2):
            round_2(way, o, False)
    round_3(0, 0, 1, True)
    for o in (0, 1):
        round_1(0, o, 1, False)
    for o in (3, 2):
        round_1(1, o, 1, False)
    round_3(1, 2, 0, True)
    round_3(1, 1, 0, True)
    round_3(0, 2, 0, True)
    flip(0, 1, 5)
    round_3(0, 1, 0, False)
    round_3(0, 1, 1, True)
    round_3(1, 3, 0, False)
    round_3(1, 3, 1, True)
    flip(0, 6, 4)
    round_3(1, 2, 0, False)
    round_3(1, 2, 1, True)
    flip(0, 10, 2)
    own_table.wait()
    table_copy.wait_recv()
    their_table = local(table_in, table.at[1])
    tile_copy.wait_recv()
    flip(1, 0, 12)
    their_table.wait()
    for way, rows in ((0, (3, 2)), (1, (1,))):
        for row in rows:
            round_3(way, row, 0, False)
    for way, rows in ((0, (0, 1)), (1, (3, 2))):
        for row in rows:
            round_3(way, row, 1, False)

    def entry(which, kind, b, s):
        return table[which, kind * 16 + b, 2 * s + core]

    def row_block(which, b):
        lhs = jnp.concatenate([swapped[which, b * SHARDS + s] for s in range(SHARDS)], axis=1)
        rhs = jnp.concatenate([gathered[entry(which, h, b, s)] for s in range(SHARDS) for h in range(2)], axis=0)
        return jnp.dot(lhs, rhs, preferred_element_type=F32)

    def rows_of(r):
        return pl.ds(pl.multiple_of(r * CHUNK, CHUNK), CHUNK)

    def edge_of(b):
        return pl.ds(pl.multiple_of(b * EDGE, EDGE), EDGE)

    def their_block(b, carry):
        theirs[edge_of(b), :] = row_block(1, b).astype(BF16)
        return carry

    def my_block(b, carry):
        mine[edge_of(b), :] = row_block(0, b)
        return carry

    def beside(dz, dy):
        return wrap(z + dz, RING) * 2 + wrap(y_lo + dy, 2)

    def share(dz, dy):
        to = beside(dz, dy)
        rows = rows_of(to)
        shares[to] = (mine[rows, :] + arrived[rows, :].astype(F32)).astype(BF16)
        return send(shares.at[to], landed.at[rep], (dom, to))

    swap, slots = [], []
    order = (2, 1, 3, 0)
    base = [wrap(z + dz, RING) for dz in order]

    def theirs_out(g):
        lax.fori_loop(base[g] * 3, base[g] * 3 + 3, their_block, 0)
        rows = pl.ds(pl.multiple_of(base[g] * 384, 384), 384)
        swap.append(send(theirs.at[rows], arrived.at[rows], partner))

    theirs_out(0)
    theirs_out(1)
    for g in range(4):
        lax.fori_loop(base[g] * 3, base[g] * 3 + 3, my_block, 0)
        if g < 2:
            theirs_out(g + 2)
        if g < 3:
            swap[g].wait_recv()
            for dy in (1, 0):
                slots.append((order[g], dy, share(order[g], dy)))
    swap[3].wait_recv()
    earlier = started[:-5]
    del started[:-5]
    slots.append((0, 1, share(0, 1)))
    for copy in earlier:
        copy.wait_send()

    total = mine[rows_of(rep), :] + arrived[rows_of(rep), :].astype(F32)
    for copy in dense_in:
        copy.wait()
    for dz, dy, copy in slots:
        copy.wait_recv()
        total = total + landed[beside(4 - dz, dy)].astype(F32)

    aggregated = total.astype(BF16)
    v = jnp.dot(aggregated, weight[...], preferred_element_type=F32) + bias[...]
    t = jnp.tanh(ROOT * (v + CUBIC * (v * v * v)))
    slope = 0.5 * (1.0 + t) + 0.5 * v * ((1.0 - t) * (1.0 + t)) * (ROOT * (1.0 + 3.0 * CUBIC * (v * v)))
    delta = (grad[...].astype(F32) * slope).astype(BF16)
    spread[0, rows_of(rep), :] = lax.dot_general(
        delta, weight[...], (((1,), (1,)), ((), ())), preferred_element_type=F32).astype(BF16)
    here = spread.at[0, rows_of(rep)]
    spread_in = {}
    for dz in (0, 1, 3, 2):
        for dy in (0, 1):
            if dz or dy:
                spread_in[dz, dy] = send(here, here, (dom, beside(dz, dy)))
    forward_in = [send(here, spread.at[1, rows_of(rep)], partner)]
    act[...] = (0.5 * v * (1.0 + t)).astype(BF16)
    outgoing = [local(act, act_out)]

    wsum = lax.dot_general(aggregated, delta, (((0,), (0,)), ((), ())), preferred_element_type=F32)
    bsum = jnp.sum(delta.astype(F32).reshape(CHUNK // 8, 8, HID), axis=0)
    for k in range(RING):
        wterm[k, 0:64, :] = wsum[k * 64:(k + 1) * 64, :]
        wterm[k, 64:72, :] = bsum
    wx[x] = wterm[x]
    w_x = [send(wterm.at[wrap(x + k, RING)], wx.at[x], near(0, k)) for k in range(1, RING)]

    for s in range(SHARDS):
        chain_own[s, NONE] = jnp.zeros((EDGE, HID), F32)
    for s in range(2):
        chain[s, NONE] = jnp.zeros((EDGE, HID), F32)

    for turn_at in range(4):
        dz = (0, 1, 3, 2)[turn_at]
        for dy in (0, 1):
            if dz or dy:
                spread_in[dz, dy].wait_recv()
                rows = rows_of(beside(4 - dz, dy))
                forward_in.append(send(spread.at[0, rows], spread.at[1, rows], partner))
        base = wrap(z + 4 - dz, RING) * 3

        def own_block(j, carry):
            b = base + j
            source = spread[0, edge_of(b), :]
            for to_x in range(4):
                product = jnp.dot(flipped[0, b, pl.ds(to_x * 2 * EDGE, 2 * EDGE), :], source, preferred_element_type=F32)
                for s in range(2):
                    prior = chain_own[to_x * 2 + s, entry(0, 2, b, s * 4 + to_x)]
                    chain_own[to_x * 2 + s, turn_at * 3 + j] = product[s * EDGE:(s + 1) * EDGE] + prior
            return carry
        lax.fori_loop(0, 3, own_block, 0)
        if turn_at == 1:
            for copy in w_x:
                copy.wait_recv()
            wx[0] = wx[0] + wx[1] + wx[2] + wx[3]
            wcore_out[0:32, :] = wx[0, pl.ds(pl.multiple_of((1 - core) * 32, 32), 32), :]
            wcore_out[32:40, :] = wx[0, 64:72, :]
            w_core = send(wcore_out, wcore, partner)
        elif turn_at == 3:
            w_core.wait_recv()
            wcore[0:32, :] = wcore[0:32, :] + wx[0, pl.ds(pl.multiple_of(core * 32, 32), 32), :]
            wcore[32:40, :] = wcore[32:40, :] + wx[0, 64:72, :]
            whi_out[0:16, :] = wcore[pl.ds(pl.multiple_of((1 - y_hi) * 16, 16), 16), :]
            whi_out[16:24, :] = wcore[32:40, :]
            w_hi = send(whi_out, whi, across)

    def link(to_x):
        rows = pl.ds(pl.multiple_of(to_x * 2 * EDGE, 2 * EDGE), 2 * EDGE)
        for turn_at in range(4):
            base = wrap(z + (0, 3, 1, 2)[turn_at], RING) * 3
            blocks = [base + j for j in range(3)]
            products = [
                jnp.dot(flipped[1, b, rows, :], spread[1, edge_of(b), :], preferred_element_type=F32) for b in blocks]
            for j, b in enumerate(blocks):
                for s in range(2):
                    prior = chain[s, entry(1, 2, b, s * 4 + to_x)]
                    chain[s, turn_at * 3 + j] = products[j][s * EDGE:(s + 1) * EDGE] + prior

    def close(to_x):
        for s in range(2):
            for c in range(BLOCKS):
                both = (chain_own[to_x * 2 + s, entry(0, 3, c, s * 4 + to_x)]
                        + chain[s, entry(1, 3, c, s * 4 + to_x)]).astype(BF16)
                for h in range(2):
                    q = 2 * c + h
                    part, r = q % 3, q // 3
                    grads[(part,) + turned(part, to_x, s * 2 + r % 2, r // 2)] = both[h * SIDE:(h + 1) * SIDE]

    off = (2, 1, 3, 0)
    to_xs = [wrap(x + d, RING) for d in off]
    to_zs = [wrap(z + d, RING) for d in off]
    slots_r = [[[[lane(2) for k in range(3)] for way in range(2)] for g in range(4)] for part in range(3)]
    ring_of = (2, 0, 1)

    def quarter(part, plane, g, h):
        if part == 0:
            return grads.at[0, plane, pl.ds(2 * h, 2), to_xs[g]]
        return grads.at[part, plane, (to_zs if part == 1 else to_xs)[g], pl.ds(2 * h, 2)]

    def land_of(part, g, way, k):
        return land_r.at[((part * 4 + g) * 2 + way) * 3 + k]

    def quarter_copy(part, g, way, k):
        axis, step = ring_of[part], (1, 3)[way]
        plane = wrap(at[axis] + (2 if k == 0 else step), RING)
        h = way if k in (0, 2) else 1 - way
        return remote(quarter(part, plane, g, h), land_of(part, g, way, k), near(axis, step), slots_r[part][g][way][k])

    def begin(copy):
        copy.start()
        started.append(copy)

    def begin_each(parts, g, k):
        for part in parts:
            for way in range(2):
                begin(quarter_copy(part, g, way, k))

    def add_to(ref, *others):
        full = ref[...].astype(F32)
        for other in others:
            full = full + other[...].astype(F32)
        ref[...] = full.astype(BF16)

    def pass_on(g):
        for part in range(3):
            for way in range(2):
                quarter_copy(part, g, way, 0).wait_recv()
                plane = wrap(at[ring_of[part]] + (1, 3)[way], RING)
                add_to(quarter(part, plane, g, way), land_of(part, g, way, 0))
                begin(quarter_copy(part, g, way, 2))

    rows_sent = {}

    def settle(g):
        for part in range(3):
            for way in range(2):
                for k in (1, 2):
                    quarter_copy(part, g, way, k).wait_recv()
            plane = at[ring_of[part]]
            for h in range(2):
                add_to(quarter(part, plane, g, h), land_of(part, g, h, 2), land_of(part, g, 1 - h, 1))
            if part == 0:
                for k in range(1, RING):
                    rows_sent[0, g, k] = send(
                        grads.at[0, z, wrap(y + k, RING), to_xs[g]], land_y.at[g * 3 + k - 1], near(1, k))
            elif g == 0:
                row, axis = (to_zs, to_xs)[part - 1][0], (2, 0)[part - 1]
                for h in range(2):
                    rows_sent[part, 0, h] = send(grads.at[part, plane, row, pl.ds(2 * h, 2)],
                                                 land_row.at[(part - 1) * 3, pl.ds(2 * h, 2)], near(axis, (1, 3)[h]))
            elif g < 3:
                row = (to_zs, to_xs)[part - 1][g]
                rows_sent[part, 0, g - 1].wait_recv()
                spot = pl.ds(2 * (g - 1), 2)
                add_to(grads.at[part, plane, row, spot], land_row.at[(part - 1) * 3, spot])
                rows_sent[part, g] = send(
                    grads.at[part, plane, row], land_row.at[(part - 1) * 3 + g], near((2, 0)[part - 1], off[g]))

    pieces_sent = {}

    def column_in(g):
        for k in range(1, RING):
            rows_sent[0, g, k].wait_recv()
        piece = grads.at[0, z, y, to_xs[g]]
        add_to(piece, *[land_y.at[g * 3 + k] for k in range(3)])
        if g < 3:
            pieces_sent[0, g] = send(piece, land_piece.at[g], near(0, off[g]))

    def row_in(part):
        for g in (1, 2):
            rows_sent[part, g].wait_recv()
        plane, row = (x, z) if part == 1 else (y, x)
        add_to(grads.at[part, plane, row], *[land_row.at[(part - 1) * 3 + g] for g in (1, 2)])
        axis = (1, 2)[part - 1]
        for g in range(3):
            pieces_sent[part, g] = send(grads.at[part, plane, row, wrap(at[axis] + off[g], RING)],
                                        land_piece.at[part * 3 + g], near(axis, off[g]))

    def piece_in(part):
        plane, row, spot = turned(part, x, y, z)
        full = grads[part, plane, row, spot].astype(F32)
        for g in range(3):
            pieces_sent[part, g].wait_recv()
            full = full + land_piece[part * 3 + g].astype(F32)
        fgrad[pl.ds(part * SIDE, SIDE), :] = full.astype(BF16)

    for copy in forward_in:
        copy.wait_recv()
    for g in range(4):
        link(to_xs[g])
        close(to_xs[g])
        begin_each((0, 2), g, 0)
        if g == 0:
            for q in range(4):
                begin_each((1,), q, 0)

    w_hi.wait_recv()
    wrep[rep, 0:16, :] = whi[0:16, :] + wcore[pl.ds(pl.multiple_of(y_hi * 16, 16), 16), :]
    wrep[rep, 16:24, :] = whi[16:24, :] + wcore[32:40, :]
    w_rep = [send(wrep.at[rep], wrep.at[rep], peer(k)) for k in range(1, REPS)]

    begin_each(range(3), 0, 1)
    pass_on(0)
    begin_each(range(3), 1, 1)
    pass_on(1)
    for copy in w_rep:
        copy.wait_recv()
    wfull = wrep[0]
    for r in range(1, REPS):
        wfull = wfull + wrep[r]
    wfull = wfull * scale
    bsum_out[...] = jnp.sum(wfull[16:24], axis=0, keepdims=True)
    outgoing.append(local(bsum_out, bgrad_out))

    def wrows(start, count):
        return wall.at[pl.ds(pl.multiple_of(start, 16), count)]

    wall[pl.ds(pl.multiple_of(x * 64 + core * 32 + y_hi * 16, 16), 16), :] = wfull[0:16]
    ref = wrows(x * 64 + core * 32 + y_hi * 16, 16)
    w_hi = send(ref, ref, across)

    begin_each(range(3), 2, 1)
    pass_on(2)
    settle(0)
    w_hi.wait_recv()
    ref = wrows(x * 64 + core * 32, 32)
    w_core = send(ref, ref, partner)

    begin_each(range(3), 3, 1)
    pass_on(3)
    settle(1)
    w_core.wait_recv()
    ref = wrows(x * 64, 64)
    w_x = [send(ref, ref, near(0, k)) for k in range(1, RING)]

    column_in(0)
    settle(2)
    column_in(1)
    settle(3)
    row_in(1)
    row_in(2)
    column_in(2)
    for copy in w_x:
        copy.wait_recv()
    outgoing.append(local(wall, wgrad_out))
    column_in(3)
    for part in (0, 1, 2):
        piece_in(part)
    outgoing.append(local(fgrad, fgrad_out))
    for copy in started:
        copy.wait_send()
    for copy in outgoing:
        copy.wait()


def hand_over(*refs):
    ins, outs, held, sems = refs[:4], refs[4:8], refs[8:12], refs[12]
    copies = [pltpu.make_async_copy(ins[k], held[k], sems.at[k]) for k in range(4)]
    for copy in copies:
        copy.start()
    onward = []
    for k in range(4):
        copies[k].wait()
        onward.append(pltpu.make_async_copy(held[k], outs[k], sems.at[4 + k]))
        onward[k].start()
    for copy in onward:
        copy.wait()


def body(features, weight, bias, adj_tiles, adj_cols, degree, grad_out):
    anywhere = pl.BlockSpec(memory_space=pl.ANY)
    rows = BLOCKS * EDGE
    scale = 1.0 / math.sqrt(CHUNK * REPS * 16)
    outs = (
        jax.ShapeDtypeStruct((CHUNK, HID), BF16),
        jax.ShapeDtypeStruct((CHUNK, HID), BF16),
        jax.ShapeDtypeStruct((HID, HID), F32),
        jax.ShapeDtypeStruct((1, HID), F32),
    )
    call = pl.pallas_call(
        lambda *refs: kernel(scale, *refs),
        out_shape=outs,
        in_specs=[anywhere] * 7,
        out_specs=(anywhere,) * 4,
        scratch_shapes=[
            pltpu.VMEM((HID, HID), BF16),
            pltpu.VMEM((1, HID), F32),
            pltpu.VMEM((BLOCKS, 1, 16), I32),
            pltpu.VMEM((BLOCKS, 16), I32),
            pltpu.VMEM((CHUNK, HID), BF16),
            pltpu.VMEM((CHUNK, HID), BF16),
            pltpu.VMEM((CHUNK, HID), BF16),
            pltpu.VMEM((2, BLOCKS * SHARDS, EDGE, EDGE), BF16),
            pltpu.VMEM((2, BLOCKS, SHARDS * EDGE, EDGE), BF16),
            pltpu.VMEM((64, 128), I32),
            pltpu.VMEM((64, 128), I32),
            pltpu.SMEM((2, 64, 128), I32),
            pltpu.VMEM((193, SIDE, HID), BF16),
            pltpu.VMEM((rows, HID), BF16),
            pltpu.VMEM((rows, HID), BF16),
            pltpu.VMEM((rows, HID), F32),
            pltpu.VMEM((REPS, CHUNK, HID), BF16),
            pltpu.VMEM((REPS, CHUNK, HID), BF16),
            pltpu.VMEM((2, rows, HID), BF16),
            pltpu.VMEM((SHARDS, 13, EDGE, HID), F32),
            pltpu.VMEM((2, 13, EDGE, HID), F32),
            pltpu.VMEM((3, 4, 4, 4, SIDE, HID), BF16),
            pltpu.VMEM((72, 2, SIDE, HID), BF16),
            pltpu.VMEM((12, SIDE, HID), BF16),
            pltpu.VMEM((6, 4, SIDE, HID), BF16),
            pltpu.VMEM((9, SIDE, HID), BF16),
            pltpu.VMEM((RING, 72, HID), F32),
            pltpu.VMEM((RING, 72, HID), F32),
            pltpu.VMEM((40, HID), F32),
            pltpu.VMEM((40, HID), F32),
            pltpu.VMEM((24, HID), F32),
            pltpu.VMEM((24, HID), F32),
            pltpu.VMEM((REPS, 24, HID), F32),
            pltpu.VMEM((HID, HID), F32),
            pltpu.VMEM((1, HID), F32),
            pltpu.SemaphoreType.DMA((640,)),
        ],
        compiler_params=pltpu.CompilerParams(
            collective_id=0, has_side_effects=True, vmem_limit_bytes=61 * 1024 * 1024),
    )
    results = call(
        features, weight, bias.reshape(1, HID),
        adj_tiles.reshape(BLOCKS * SHARDS, 2, EDGE, EDGE), adj_cols.transpose(0, 2, 1), degree, grad_out)
    act, fgrad, wgrad, bgrad = pl.pallas_call(
        hand_over,
        out_shape=outs,
        in_specs=[anywhere] * 4,
        out_specs=(anywhere,) * 4,
        scratch_shapes=[pltpu.VMEM(out.shape, out.dtype) for out in outs] + [pltpu.SemaphoreType.DMA((8,))],
    )(*results)
    return act, fgrad, wgrad, bgrad.reshape(HID)


def solution(mesh):
    return jax.shard_map(
        body,
        mesh=mesh,
        in_specs=(
            P(("dom", "rep"), None),
            P(),
            P(),
            P("dom", None, "rep", None, None),
            P("dom", None, "rep"),
            P("dom", None),
            P(("dom", "rep"), None),
        ),
        out_specs=(P(("dom", "rep"), None), P(("dom", "rep"), None), P(), P()),
        check_vma=False,
    )
```
